256 devices in a mesh: ctx: 16 (over z, core), head: 16 (over x, y).
Axes of the slice: x: 4, y: 4, z: 8, core: 2. Of those that a mesh axis runs over, the one named last changes fastest.
Arguments:
- q_rows: bfloat16 [8192, 2048], P('ctx', 'head'), may hold values from -6 to 6
- k_rows: bfloat16 [8192, 2048], P('ctx', 'head'), may hold values from -6 to 6
- v_rows: bfloat16 [8192, 4096], P('ctx', 'head'), may hold values from -6 to 6
- gate_rows: bfloat16 [8192, 4096], P('ctx', 'head'), may hold values from -6 to 6
- beta_logits: bfloat16 [8192, 32], P('ctx', 'head'), may hold values from -10 to 4
- log_decay: bfloat16 [8192, 32], P('ctx', 'head'), may hold values from -0.7 to 0
- norm_gain: float32 [128], replicated, may hold values from 0.1 to 1.9
- out_weight: bfloat16 [4096, 2048], P('head'), may hold values from -0.09375 to 0.09375
- prompt_blocks: int32 [8], replicated, may hold values from 1 to 32, as said below
- arrival_slot: int32 [64], replicated, may hold values from 0 to 63, as said below
Outputs:
- layer_out: bfloat16 [8192, 2048], P(('ctx', 'head'))
The draws below stay inside these ranges and needn't reach their ends.
Inputs may be any that keep to these rules, and one draw needn't show every extreme that they name: A permutation; block b arrives at ctx index arrival_slot[b] // 4, and the blocks of ctx index c in stream order are c * 4 to c * 4 + 3. Every ctx index receives at most 2 of its blocks from one ctx index, and exactly 2 from some. `prompt_blocks`: the last prompt has exactly 32 blocks.
All inputs are finite; a program needn't handle non-finite values.
Results may differ from the reference program's by a relative error of at most 0.0049.
Values may be sent and summed in bfloat16 or wider, within the bound.
A program may use at most 128 MiB of HBM per device.

```python
import jax
import jax.numpy as jnp
import numpy as np
from jax import lax

D = 2048
HK = 16
HV = 32
DK = 128
DV = 128
SPAN = 128
PROMPTS = 8
TOKEN_TOTAL = 8192
BLOCK_DEV = 4
BLOCKS = 64
CAP = 2
LONGEST = 32


def draw_arrival_slot(key, part):
    key = jax.random.fold_in(key, 11)
    peers = BLOCKS // BLOCK_DEV
    extra_total = BLOCK_DEV - CAP
    base = extra_total // (peers - 1)
    leftover = extra_total % (peers - 1)
    counts = np.array([CAP] + [base + (1 if j < leftover else 0) for j in range(peers - 1)])
    column_of_rank = jnp.asarray(np.repeat(np.arange(peers), counts).astype(np.int32))
    first, second, third, fourth, fifth = jax.random.split(key, 5)
    row_labels = jax.random.permutation(first, peers).astype(jnp.int32)
    source_labels = jax.random.permutation(second, peers).astype(jnp.int32)
    column_labels = jax.random.permutation(third, peers).astype(jnp.int32)
    dest_keys = jax.random.split(fourth, peers)
    ranks = jax.vmap(lambda single: jax.random.permutation(single, BLOCK_DEV))(dest_keys).reshape(-1).astype(jnp.int32)
    dests = jnp.arange(BLOCKS, dtype=jnp.int32) // BLOCK_DEV
    columns = column_of_rank[ranks]
    sources = source_labels[(row_labels[dests] + column_labels[columns]) % peers]
    tie_break = jax.random.permutation(fifth, BLOCKS).astype(jnp.int32)
    score = sources * BLOCKS + tie_break
    order = jnp.argsort(score)
    return jnp.argsort(order).astype(jnp.int32)


def draw_prompt_blocks(key, part):
    key = jax.random.fold_in(key, 13)
    cuts = jax.random.permutation(key, LONGEST - 1).astype(jnp.int32) + 1
    chosen = jnp.sort(cuts[:PROMPTS - 2])
    edges = jnp.concatenate([jnp.zeros((1,), jnp.int32), chosen, jnp.full((1,), LONGEST, jnp.int32)])
    others = edges[1:] - edges[:-1]
    return jnp.concatenate([others, jnp.full((1,), LONGEST, jnp.int32)]).astype(jnp.int32)


def draw_beta_logits(key, part):
    key = jax.random.fold_in(key, 5)
    first, second = jax.random.split(key)
    offsets = jax.random.uniform(first, (HV,), jnp.float32, -7.0, 1.0)
    noise = jnp.clip(jax.random.normal(second, (TOKEN_TOTAL, HV), jnp.float32), -3.0, 3.0)
    return (offsets[None, :] + noise).astype(jnp.bfloat16)


def draw_log_decay(key, part):
    key = jax.random.fold_in(key, 7)
    first, second, third, fourth = jax.random.split(key, 4)
    decay_rates = jnp.exp(jax.random.uniform(first, (HV,), jnp.float32, -11.5, -3.0))
    approximate_output = jax.random.uniform(second, (TOKEN_TOTAL, HV), jnp.float32, 0.5, 2.0)
    arrival_places = jax.random.randint(third, (4,), 0, TOKEN_TOTAL)
    arrival_group = jnp.any(jnp.arange(TOKEN_TOTAL)[:, None] == arrival_places[None, :], axis=1)
    dropped_rows = jax.random.uniform(fourth, (HV,), jnp.float32, 0.2, 0.5)
    value_rows = jnp.where(arrival_group[:, None], jnp.log(1.0 - dropped_rows)[None, :], -decay_rates[None, :] * approximate_output)
    return value_rows.astype(jnp.bfloat16)


def levels(key, shape, pieces, low, largest):
    gain, own = 1.0, jax.random.fold_in(key, 6)
    for axis_at, blocks in pieces:
        steps = jnp.exp(jax.random.uniform(jax.random.fold_in(own, axis_at), (blocks,), jnp.float32, low / len(pieces), largest / len(pieces)))
        gain = gain * jnp.repeat(steps, shape[axis_at] // blocks).reshape([-1 if axis == axis_at else 1 for axis in range(len(shape))])
    return gain


def normal_values(own_key, extent, scale, reach, cuts=(), kind=jnp.bfloat16):
    result = scale * jax.random.normal(own_key, extent, jnp.float32)
    if cuts:
        result = result * levels(own_key, extent, cuts, -0.22, 0.18)
    return jnp.clip(result, -reach, reach).astype(kind)


def setup_inputs(seed: int = 0) -> dict:
    key_list = jax.random.split(jax.random.key(seed), 11)
    return {
        "q_rows": normal_values(key_list[0], (TOKEN_TOTAL, HK * DK), 1.0, 6.0, ((0, 16), (1, 16))),
        "k_rows": normal_values(key_list[1], (TOKEN_TOTAL, HK * DK), 1.0, 6.0, ((0, 16), (1, 16))),
        "v_rows": normal_values(key_list[2], (TOKEN_TOTAL, HV * DV), 1.0, 6.0, ((0, 16), (1, 16))),
        "gate_rows": normal_values(key_list[3], (TOKEN_TOTAL, HV * DV), 1.0, 6.0, ((0, 16), (1, 16))),
        "beta_logits": draw_beta_logits(jax.random.fold_in(key_list[10], 71), 0),
        "log_decay": draw_log_decay(jax.random.fold_in(key_list[10], 71), 0),
        "norm_gain": jnp.clip(1.0 + 0.18 * jax.random.normal(key_list[6], (DV,), jnp.float32), 0.1, 1.9),
        "out_weight": normal_values(key_list[7], (HV * DV, D), (HV * DV) ** -0.5, 0.09375, ((0, 16),)),
        "prompt_blocks": draw_prompt_blocks(jax.random.fold_in(key_list[10], 71), 0),
        "arrival_slot": draw_arrival_slot(jax.random.fold_in(key_list[10], 71), 0),
    }


def unit_rows(value_rows):
    return value_rows * lax.rsqrt(lax.optimization_barrier(jnp.sum(value_rows * value_rows, axis=-1, keepdims=True)) + 1e-06)

def matrix_product(form, left, right):
    return jnp.einsum(form, left, right, precision=lax.Precision.HIGHEST)

def span_terms(queries, keys_in, value_rows, beta, decay):
    width = queries.shape[0]
    row_ids = jnp.arange(width, dtype=jnp.int32)
    incl = row_ids[:, None] >= row_ids[None, :]
    strict = row_ids[:, None] > row_ids[None, :]
    cumulative = jnp.cumsum(decay)
    spread = cumulative[:, None] - cumulative[None, :]
    ratio = jnp.where(incl, jnp.exp(jnp.where(incl, spread, 0.0)), 0.0)
    key_key = matrix_product('ik,jk->ij', keys_in, keys_in)
    lower = jnp.where(strict, beta[:, None] * ratio * key_key, 0.0)
    growth = jnp.exp(cumulative)
    rhs = jnp.concatenate([beta[:, None] * value_rows, (beta * growth)[:, None] * keys_in], axis=1)
    solved = jax.scipy.linalg.solve_triangular(jnp.eye(width, dtype=jnp.float32) + lower, rhs, lower=True, unit_diagonal=True)
    w_value = solved[:, :value_rows.shape[1]]
    w_key = solved[:, value_rows.shape[1]:]
    attend = ratio * matrix_product('ik,jk->ij', queries, keys_in)
    local_output = matrix_product('ij,jv->iv', attend, w_value)
    query_lookup = growth[:, None] * queries - matrix_product('ij,jk->ik', attend, w_key)
    tail = jnp.exp(cumulative[-1] - cumulative)[:, None] * keys_in
    transit = jnp.exp(cumulative[-1]) * jnp.eye(keys_in.shape[1], dtype=jnp.float32) - matrix_product('jk,jl->kl', tail, w_key)
    offset = matrix_product('jk,jv->kv', tail, w_value)
    return (query_lookup, local_output, transit, offset)

def reference(q_rows, k_rows, v_rows, gate_rows, beta_logits, log_decay, norm_gain, out_weight, prompt_blocks, arrival_slot):

    def stream(rows):
        return rows.reshape(BLOCKS, SPAN, -1)[arrival_slot]
    ratio_heads = HV // HK
    queries = unit_rows(stream(q_rows).astype(jnp.float32).reshape(BLOCKS, SPAN, HK, DK)) * DK ** (-0.5)
    keys_all = unit_rows(stream(k_rows).astype(jnp.float32).reshape(BLOCKS, SPAN, HK, DK))
    queries = jnp.repeat(queries, ratio_heads, axis=2)
    keys_all = jnp.repeat(keys_all, ratio_heads, axis=2)
    value_rows = stream(v_rows).astype(jnp.float32).reshape(BLOCKS, SPAN, HV, DV)
    gates = stream(gate_rows).astype(jnp.float32).reshape(BLOCKS, SPAN, HV, DV)
    beta = jax.nn.sigmoid(stream(beta_logits).astype(jnp.float32))
    decay = stream(log_decay).astype(jnp.float32)
    starts = jnp.cumsum(prompt_blocks) - prompt_blocks
    is_start = jnp.any(jnp.arange(BLOCKS, dtype=jnp.int32)[:, None] == starts[None, :], axis=1)
    keep = jnp.where(is_start, 0.0, 1.0).astype(jnp.float32)
    head_terms = jax.vmap(span_terms, in_axes=(1, 1, 1, 1, 1))

    def step(running_state, inputs):
        query_block, key_b, value_b, beta_b, decay_b, gate_b, keep_b = inputs
        query_lookup, local_output, transit, offset = head_terms(query_block, key_b, value_b, beta_b, decay_b)
        running_state = keep_b * running_state
        delta_kernel = matrix_product('egu,euq->egq', query_lookup, running_state) + local_output
        running_state = matrix_product('hij,hjv->hiv', transit, running_state) + offset
        delta_kernel = jnp.transpose(delta_kernel, (1, 0, 2))
        scale = lax.rsqrt(lax.optimization_barrier(jnp.mean(delta_kernel * delta_kernel, axis=-1, keepdims=True)) + 1e-06)
        normed = (delta_kernel * scale * norm_gain * jax.nn.silu(gate_b)).astype(jnp.bfloat16)
        return (running_state, normed.reshape(SPAN, HV * DV))
    start_state = jnp.zeros((HV, DK, DV), jnp.float32)
    _, normed_all = lax.scan(step, start_state, (queries, keys_all, value_rows, beta, decay, gates, keep))
    order = jnp.argsort(arrival_slot).astype(jnp.int32)
    arrived = normed_all[order].reshape(TOKEN_TOTAL, HV * DV)
    return jnp.dot(arrived.astype(jnp.float32), out_weight.astype(jnp.float32), preferred_element_type=jnp.float32).astype(jnp.bfloat16)
```

```python
import jax
import jax.numpy as jnp
from jax import lax
from jax.experimental import pallas as pl
from jax.experimental.pallas import tpu as pltpu
from jax.sharding import PartitionSpec as P

SPAN = 128
DK = 128
DV = 128
HEADS = 2
LOCAL = 4
PEERS = 16
CHIPS = 8
SLICE = 16
BLOCKS = 64
CHAIN = 32
SIDE = 4
MODEL = 2048
PIECES = 4
PIECE = MODEL // PIECES
GROUP = 2
VMEM_LIMIT = 60 * 2**20
MESH = pl.DeviceIdType.MESH
F32 = jnp.float32
BF16 = jnp.bfloat16


def split(x):
    high = x.astype(BF16)
    return high, (x - high.astype(F32)).astype(BF16)


def mm(a, b):
    return jnp.dot(a, b, preferred_element_type=F32)


def mm_t(a, b):
    return lax.dot_general(a, b, (((1,), (1,)), ((), ())), preferred_element_type=F32)


def product(a, b):
    a_high, a_low = a
    b_high, b_low = b
    n = b_high.shape[1]
    if n == 128:
        left = jnp.concatenate([a_high, a_low], axis=1)
        right = jnp.concatenate(
            [
                jnp.concatenate([b_high, b_low], axis=1),
                jnp.concatenate([b_high, jnp.zeros_like(b_low)], axis=1),
            ],
            axis=0,
        )
        both = mm(left, right)
        return both[:, :n] + both[:, n:]
    left = jnp.concatenate([a_high, a_low], axis=1)
    right = jnp.concatenate([b_high, b_high], axis=0)
    return mm(left, right) + mm(a_high, b_low)


def spread_lanes(column):
    return jnp.broadcast_to(column, (column.shape[0], 128))


def block_terms(i, h, q, k, beta_row, decay_row, v, shared, consts):
    tri, strict, incl = consts
    qn, kf, kt2, rk_wide, kk, qk = shared
    beta = jnp.broadcast_to(1.0 / (1.0 + jnp.exp(-beta_row)), (SPAN, SPAN)).T
    steps = jnp.broadcast_to(decay_row, (SPAN, SPAN)).astype(BF16)
    wide = mm_t(tri, steps)
    wide_row = mm_t(steps, tri)
    ratio = jnp.exp(jnp.minimum(wide - wide_row, 0.0))
    lower = jnp.where(strict, beta * ratio * kk, 0.0)
    attend = jnp.where(incl, ratio * qk, 0.0)
    growth = jnp.exp(wide)
    end = wide[SPAN - 1 : SPAN, :]
    tail = jnp.exp(end - wide) * rk_wide
    rhs = jnp.concatenate([beta * v, beta * growth * rk_wide * kf], axis=1)
    return dict(i=i, h=h, lower=lower, attend=attend, tail=tail, rhs=rhs, kt2=kt2, grown=growth * qn, decay=jnp.exp(end))


def main_kernel(
    arr_ref, prompt_ref, q_hbm, k_hbm, v_hbm, gate_hbm, beta_hbm, decay_hbm, gain_hbm, w_ref,
    out_ref,
    q_ref, k_ref, v_ref, gate_ref, beta_ref, decay_ref, gain_ref,
    m_ref, o_ref, d_ref, ql_ref, lo_ref, inv_vmem, inv_ref,
    m_all, o_all, d_all, stream, states, entry, normed, rows_all, w_all, part, got,
    in_sem, inv_sem, w_send, w_recv, w_local, c_send, c_recv, m_send, m_recv, o_send, o_recv, d_send, d_recv,
    s_send, s_recv, n_send, n_recv, p_send, p_recv,
):
    ctx = lax.axis_index("ctx")
    head = lax.axis_index("head")
    chip, core = lax.div(ctx, 2), lax.rem(ctx, 2)
    sibling = 2 * chip + 1 - core
    side_x, side_y = lax.div(head, SIDE), lax.rem(head, SIDE)

    def ctx_peer(k):
        return lax.rem(ctx + k, PEERS)

    def y_peer(k):
        return side_x * SIDE + lax.rem(side_y + k, SIDE)

    def x_peer(k):
        return lax.rem(side_x + k, SIDE) * SIDE + side_y

    barrier = pltpu.get_barrier_semaphore()

    def greet(k, carry):
        pl.semaphore_signal(barrier, inc=1, device_id=(ctx_peer(k), head), device_id_type=MESH)
        return carry

    loads = [
        pltpu.make_async_copy(src, dst, in_sem.at[n])
        for n, (src, dst) in enumerate(
            (
                (k_hbm, k_ref), (q_hbm, q_ref), (beta_hbm, beta_ref), (decay_hbm, decay_ref),
                (v_hbm, v_ref), (gate_hbm, gate_ref), (gain_hbm, gain_ref),
            )
        )
    ]
    for load in loads:
        load.start()
    lax.fori_loop(1, PEERS, greet, 0)
    for k in range(1, SIDE):
        pl.semaphore_signal(barrier, inc=1, device_id=(ctx, y_peer(k)), device_id_type=MESH)
        pl.semaphore_signal(barrier, inc=1, device_id=(ctx, x_peer(k)), device_id_type=MESH)

    def remote(src, dst, send, recv, target):
        return pltpu.make_async_remote_copy(
            src_ref=src, dst_ref=dst, send_sem=send, recv_sem=recv, device_id=target, device_id_type=MESH
        )

    def o_copy(k):
        to = ctx_peer(k)
        return remote(
            o_ref.at[lax.rem(to, 2), lax.div(to, 2)], o_all.at[pl.ds(LOCAL * ctx, LOCAL)],
            o_send.at[k], o_recv.at[k], (to, head),
        )

    def d_copy(k):
        return remote(
            d_ref, d_all.at[pl.ds(pl.multiple_of(8 * ctx, 8), 8)],
            d_send.at[k], d_recv.at[k], (ctx_peer(k), head),
        )

    def m_slot(source, g):
        return m_all.at[pl.ds(LOCAL * source + GROUP * g, GROUP)]

    def m_near(z):
        return lax.rem(chip + z + CHIPS, CHIPS)

    def m_first(h, step, g, n):
        return remote(
            m_ref.at[h, pl.ds(GROUP * g, GROUP)], m_slot(ctx, g), m_send.at[n], m_recv.at[2 * ctx + g],
            (2 * m_near(step) + h, head),
        )

    def m_sibling(g, n):
        return remote(
            m_ref.at[1 - core, pl.ds(GROUP * g, GROUP)], m_slot(ctx, g), m_send.at[n], m_recv.at[2 * ctx + g],
            (sibling, head),
        )

    def m_next(source, g, step, n):
        return remote(
            m_slot(source, g), m_slot(source, g), m_send.at[n], m_recv.at[2 * source + g],
            (2 * m_near(step) + core, head),
        )

    def w_half(half):
        return w_ref.at[:, pl.ds(pl.multiple_of(half * (MODEL // 2), MODEL // 2), MODEL // 2)]

    def w_copy(k):
        return remote(w_half(core), w_all.at[core, side_y], w_send.at[k], w_recv.at[k], (ctx, y_peer(k)))

    def w_pass(k):
        slot = w_all.at[core, lax.rem(side_y + k, SIDE)]
        return remote(slot, slot, c_send.at[k], c_recv.at[k], (sibling, head))

    row = lax.broadcasted_iota(jnp.int32, (SPAN, SPAN), 0)
    col = lax.broadcasted_iota(jnp.int32, (SPAN, SPAN), 1)
    differ = row ^ col
    incl = row >= col
    strict = row > col
    tri = incl.astype(F32).astype(BF16)
    masks = [((differ >= s) & (differ < 2 * s)).astype(F32).astype(BF16) for s in (2, 4, 8, 16, 32, 64)]
    first = (differ == 1).astype(F32)
    eye = (row == col).astype(F32)
    sent = []
    everything = []

    for load in loads[:5]:
        load.wait()
    for g in range(LOCAL // GROUP):
        chains = []
        for i in range(g * GROUP, (g + 1) * GROUP):
            rows = pl.ds(i * SPAN, SPAN)
            q = q_ref[rows, :]
            k = k_ref[rows, :]
            qf = q.astype(F32)
            kf = k.astype(F32)
            rq = lax.rsqrt(jnp.sum(qf * qf, axis=-1, keepdims=True) + 1e-6) * DK**-0.5
            rk = lax.rsqrt(jnp.sum(kf * kf, axis=-1, keepdims=True) + 1e-6)
            rk_wide = spread_lanes(rk)
            rk_row = rk_wide.T
            both = mm_t(jnp.concatenate([k, q], axis=0), k)
            kk = both[:SPAN] * rk_wide * rk_row
            qk = both[SPAN:] * spread_lanes(rq) * rk_row
            kt = k.T
            shared = (qf * rq, kf, jnp.concatenate([kt, kt], axis=1), rk_wide, kk, qk)
            logits = beta_ref[:, rows].astype(F32)
            decays = decay_ref[:, rows].astype(F32)
            for h in range(HEADS):
                chains.append(
                    block_terms(
                        i, h, q, k, logits[h : h + 1], decays[h : h + 1],
                        v_ref[rows, h * DV : (h + 1) * DV].astype(F32), shared, (tri, strict, incl),
                    )
                )
        for c in chains:
            c["parts"] = split(c["lower"])
            c["inverse"] = eye - c["lower"] * first
        for mask in masks:
            for c in chains:
                c["halves"] = split(c["inverse"])
                off = (c["parts"][0] * mask, c["parts"][1] * mask)
                c["inner"] = product(off, c["halves"])
            for c in chains:
                c["inverse"] = c["inverse"] - product(c["halves"], split(c["inner"]))
        for c in chains:
            c["solved"] = product(split(c["inverse"]), split(c["rhs"]))
        for c in chains:
            tail2 = jnp.concatenate([c["tail"], c["tail"]], axis=1)
            high, low = split(tail2 * c["solved"])
            shift = mm(c["kt2"], jnp.concatenate([high, low], axis=0))
            i, h = c["i"], c["h"]
            m_ref[h, i] = shift[:, DV:].astype(BF16)
            o_ref[h, :, i] = shift[:, :DV].T.reshape(CHIPS, SLICE, DK).astype(BF16)
            d_ref[h * LOCAL + i : h * LOCAL + i + 1, :] = c["decay"]
        everything += chains
        if g == 0:
            pl.semaphore_wait(barrier, PEERS - 1 + 2 * (SIDE - 1))
        firsts = [m_first(h, step, g, g * 5 + n) for n, (h, step) in enumerate(((0, 1), (0, -1), (1, 1), (1, -1)))]
        firsts.append(m_sibling(g, g * 5 + 4))
        for copy in firsts:
            copy.start()
        sent += firsts
        if g == 0:
            for k in range(1, SIDE):
                copy = w_copy(k)
                copy.start()
                sent.append(copy)
            w_own = [
                pltpu.make_async_copy(w_half(half), w_all.at[half, side_y], w_local.at[half]) for half in range(2)
            ]
            for copy in w_own:
                copy.start()

    def send_small(k, carry):
        d_copy(k).start()
        o_copy(k).start()
        return carry

    lax.fori_loop(1, PEERS, send_small, 0)
    m_all[pl.ds(LOCAL * ctx, LOCAL)] = m_ref[core]
    o_all[pl.ds(LOCAL * ctx, LOCAL)] = o_ref[core, chip]
    d_all[pl.ds(pl.multiple_of(8 * ctx, 8), 8), :] = d_ref[...]

    lanes = lax.broadcasted_iota(jnp.int32, (1, SPAN), 1)
    found = jnp.zeros((1, SPAN), jnp.int32)
    for t in range(BLOCKS):
        found = jnp.where(lanes == arr_ref[t], t, found)
    inv_vmem[...] = found
    inv_copy = pltpu.make_async_copy(inv_vmem, inv_ref, inv_sem)
    inv_copy.start()
    bits = jnp.int32(0)
    start = prompt_ref[0]
    for i in range(1, 7):
        bits = bits | (jnp.int32(1) << start)
        start = start + prompt_ref[i]

    for c in everything:
        i, h = c["i"], c["h"]
        local = product(split(c["attend"]), split(c["solved"]))
        lo_ref[h, i] = local[:, :DV]
        ql_ref[h, i] = c["grown"] - local[:, DV:]

    n = 10
    for k in range(1, 5):
        for g in range(LOCAL // GROUP):
            for step in (1, -1):
                for s in range(2):
                    last = 4 if (s == 0) == (step == 1) else 3
                    if k > last:
                        continue
                    source = 2 * m_near(-step * k) + s
                    m_next(source, g, step, 0).wait_recv()
                    if k < last:
                        copy = m_next(source, g, step, n)
                        copy.start()
                        sent.append(copy)
                        n += 1
    for g in range(LOCAL // GROUP):
        m_next(sibling, g, 0, 0).wait_recv()

    def wait_small(k, carry):
        d_copy(k).wait()
        o_copy(k).wait()
        return carry

    lax.fori_loop(1, PEERS, wait_small, 0)
    inv_copy.wait()

    def advance(state, t):
        slot = arr_ref[t]
        stream[t] = state.astype(BF16)
        high, low = split(state)
        moved = mm_t(jnp.concatenate([high, low], axis=0), m_all[slot])
        decay = d_all[pl.ds(lax.div(slot, LOCAL) * 8 + core * LOCAL + lax.rem(slot, LOCAL), 1), :]
        return decay * state - moved[:SLICE] - moved[SLICE:] + o_all[slot].astype(F32)

    def step(t, pair):
        keep = (1 - ((bits >> t) & 1)).astype(F32)
        return advance(keep * pair[0], t), advance(pair[1], t + CHAIN)

    empty = jnp.zeros((SLICE, DK), F32)
    lax.fori_loop(0, CHAIN, step, (empty, empty), unroll=4)

    def place(a, carry):
        states[a] = stream[inv_ref[0, a]]
        return carry

    lax.fori_loop(0, BLOCKS, place, 0, unroll=8)

    def s_rows(h, z):
        return entry.at[h, :, pl.ds(pl.multiple_of(SLICE * z, SLICE), SLICE), :]

    def s_copy(k):
        to = ctx_peer(k)
        return remote(
            states.at[pl.ds(LOCAL * to, LOCAL)], s_rows(core, chip), s_send.at[k], s_recv.at[k], (to, head)
        )

    def s_arrival(k):
        source = lax.rem(ctx - k + PEERS, PEERS)
        return remote(
            states.at[pl.ds(0, LOCAL)], s_rows(lax.rem(source, 2), lax.div(source, 2)),
            s_send.at[k], s_recv.at[k], (ctx, head),
        )

    def send_states(k, carry):
        s_copy(k).start()
        return carry

    lax.fori_loop(1, PEERS, send_states, 0)
    entry[core, :, pl.ds(pl.multiple_of(SLICE * chip, SLICE), SLICE), :] = states[pl.ds(LOCAL * ctx, LOCAL)]
    for copy in w_own:
        copy.wait()
    for k in range(1, SIDE):
        w_copy(SIDE - k).wait_recv()
        copy = w_pass(k)
        copy.start()
        sent.append(copy)
    for load in loads[5:]:
        load.wait()

    def wait_states(k, carry):
        s_copy(k).wait_send()
        s_arrival(k).wait_recv()
        return carry

    lax.fori_loop(1, PEERS, wait_states, 0)

    gain = gain_ref[...]
    for i in range(LOCAL):
        for h in range(HEADS):
            high, low = split(ql_ref[h, i])
            state = entry[h, i]
            both = mm_t(jnp.concatenate([high, low], axis=0), state)
            core_out = both[:SPAN] + both[SPAN:] + lo_ref[h, i]
            scale = lax.rsqrt(jnp.mean(core_out * core_out, axis=-1, keepdims=True) + 1e-6)
            gate = gate_ref[i * SPAN : (i + 1) * SPAN, h * DV : (h + 1) * DV].astype(F32)
            value = core_out * scale * gain * (gate / (1.0 + jnp.exp(-gate)))
            normed[i, :, :, h * DV : (h + 1) * DV] = value.astype(BF16).reshape(SIDE, 32, DV)

    def n_copy(k):
        return remote(
            normed.at[:, lax.rem(side_y + k, SIDE)], rows_all.at[side_y], n_send.at[k], n_recv.at[k], (ctx, y_peer(k))
        )

    for k in range(1, SIDE):
        copy = n_copy(k)
        copy.start()
        sent.append(copy)
    rows_all[side_y] = normed[:, side_y]
    for k in range(1, SIDE):
        w_pass(k).wait_recv()
    for k in range(1, SIDE):
        n_copy(k).wait_recv()

    def p_copy(piece, k):
        return remote(
            part.at[piece, lax.rem(side_x + k, SIDE)], got.at[piece, k],
            p_send.at[piece * SIDE + k], p_recv.at[piece * SIDE + k], (ctx, x_peer(k)),
        )

    left = jnp.concatenate(
        [rows_all[y].reshape(SPAN, HEADS * DV) for y in range(SIDE)], axis=1
    )
    for piece in range(PIECES):
        half, off = divmod(piece * PIECE, MODEL // 2)
        right = w_all[half, :, :, off : off + PIECE].reshape(SIDE * HEADS * DV, PIECE)
        total = mm(left, right)
        part[piece] = total.astype(BF16).reshape(SIDE, 32, PIECE)
        for k in range(1, SIDE):
            copy = p_copy(piece, k)
            copy.start()
            sent.append(copy)
    for piece in range(PIECES):
        total = part[piece, side_x].astype(F32)
        for k in range(1, SIDE):
            p_copy(piece, k).wait_recv()
            total = total + got[piece, k].astype(F32)
        out_ref[:, piece * PIECE : (piece + 1) * PIECE] = total.astype(BF16)
    for copy in sent:
        copy.wait_send()


def per_device(q_rows, k_rows, v_rows, gate_rows, beta_logits, log_decay, norm_gain, out_weight, prompt_blocks, arrival_slot):
    smem = pl.BlockSpec(memory_space=pltpu.SMEM)
    vmem = pl.BlockSpec(memory_space=pltpu.VMEM)
    whole = pl.BlockSpec(memory_space=pl.ANY)
    tokens = LOCAL * SPAN
    dma = pltpu.SemaphoreType.DMA
    return pl.pallas_call(
        main_kernel,
        out_shape=jax.ShapeDtypeStruct((tokens // PEERS, MODEL), BF16),
        in_specs=[smem, smem] + [whole] * 8,
        out_specs=vmem,
        scratch_shapes=[
            pltpu.VMEM((tokens, DK), BF16),
            pltpu.VMEM((tokens, DK), BF16),
            pltpu.VMEM((tokens, HEADS * DV), BF16),
            pltpu.VMEM((tokens, HEADS * DV), BF16),
            pltpu.VMEM((HEADS, tokens), BF16),
            pltpu.VMEM((HEADS, tokens), BF16),
            pltpu.VMEM((1, DV), F32),
            pltpu.VMEM((HEADS, LOCAL, DK, DK), BF16),
            pltpu.VMEM((HEADS, CHIPS, LOCAL, SLICE, DK), BF16),
            pltpu.VMEM((HEADS * LOCAL, DK), F32),
            pltpu.VMEM((HEADS, LOCAL, SPAN, DK), F32),
            pltpu.VMEM((HEADS, LOCAL, SPAN, DV), F32),
            pltpu.VMEM((1, SPAN), jnp.int32),
            pltpu.SMEM((1, SPAN), jnp.int32),
            pltpu.VMEM((BLOCKS, DK, DK), BF16),
            pltpu.VMEM((BLOCKS, SLICE, DK), BF16),
            pltpu.VMEM((PEERS * HEADS * LOCAL, DK), F32),
            pltpu.VMEM((BLOCKS, SLICE, DK), BF16),
            pltpu.VMEM((BLOCKS, SLICE, DK), BF16),
            pltpu.VMEM((HEADS, LOCAL, DV, DK), BF16),
            pltpu.VMEM((LOCAL, SIDE, 32, HEADS * DV), BF16),
            pltpu.VMEM((SIDE, LOCAL, 32, HEADS * DV), BF16),
            pltpu.VMEM((2, SIDE, HEADS * DV, MODEL // 2), BF16),
            pltpu.VMEM((PIECES, SIDE, 32, PIECE), BF16),
            pltpu.VMEM((PIECES, SIDE, 32, PIECE), BF16),
            dma((7,)), dma, dma((SIDE,)), dma((SIDE,)), dma((2,)), dma((SIDE,)), dma((SIDE,)),
            dma((30,)), dma((2 * PEERS,)),
            dma((PEERS,)), dma((PEERS,)), dma((PEERS,)), dma((PEERS,)),
            dma((PEERS,)), dma((PEERS,)), dma((SIDE,)), dma((SIDE,)),
            dma((PIECES * SIDE,)), dma((PIECES * SIDE,)),
        ],
        compiler_params=pltpu.CompilerParams(
            collective_id=0, has_side_effects=True, vmem_limit_bytes=VMEM_LIMIT
        ),
    )(
        arrival_slot, prompt_blocks, q_rows, k_rows, v_rows, gate_rows, beta_logits.T, log_decay.T,
        norm_gain.reshape(1, DV), out_weight,
    )


def solution(mesh):
    in_specs = (
        P("ctx", "head"),
        P("ctx", "head"),
        P("ctx", "head"),
        P("ctx", "head"),
        P("ctx", "head"),
        P("ctx", "head"),
        P(),
        P("head", None),
        P(),
        P(),
    )
    return jax.shard_map(
        per_device, mesh=mesh, in_specs=in_specs, out_specs=P(("ctx", "head"), None), check_vma=False
    )
```

```python
import jax
import jax.numpy as jnp
from jax import lax
from jax.experimental import pallas as pl
from jax.experimental.pallas import tpu as pltpu
from jax.sharding import PartitionSpec as P

SPAN = 128
DK = 128
DV = 128
HEADS = 2
LOCAL = 4
PEERS = 16
CHIPS = 8
SLICE = 16
BLOCKS = 64
CHAIN = 32
SIDE = 4
MODEL = 2048
PIECES = 4
PIECE = MODEL // PIECES
GROUP = 2
VMEM_LIMIT = 60 * 2**20
MESH = pl.DeviceIdType.MESH
F32 = jnp.float32
BF16 = jnp.bfloat16


def split(x):
    high = x.astype(BF16)
    return high, (x - high.astype(F32)).astype(BF16)


def mm(a, b):
    return jnp.dot(a, b, preferred_element_type=F32)


def mm_t(a, b):
    return lax.dot_general(a, b, (((1,), (1,)), ((), ())), preferred_element_type=F32)


def product(a, b):
    a_high, a_low = a
    b_high, b_low = b
    n = b_high.shape[1]
    if n == 128:
        left = jnp.concatenate([a_high, a_low], axis=1)
        right = jnp.concatenate(
            [
                jnp.concatenate([b_high, b_low], axis=1),
                jnp.concatenate([b_high, jnp.zeros_like(b_low)], axis=1),
            ],
            axis=0,
        )
        both = mm(left, right)
        return both[:, :n] + both[:, n:]
    left = jnp.concatenate([a_high, a_low], axis=1)
    right = jnp.concatenate([b_high, b_high], axis=0)
    return mm(left, right) + mm(a_high, b_low)


def spread_lanes(column):
    return jnp.broadcast_to(column, (column.shape[0], 128))


def block_terms(i, h, q, k, beta_row, decay_row, v, shared, consts):
    tri, strict, incl = consts
    qn, kf, kt2, rk_wide, kk, qk = shared
    beta = jnp.broadcast_to(1.0 / (1.0 + jnp.exp(-beta_row)), (SPAN, SPAN)).T
    steps = jnp.broadcast_to(decay_row, (SPAN, SPAN)).astype(BF16)
    wide = mm_t(tri, steps)
    wide_row = mm_t(steps, tri)
    ratio = jnp.exp(jnp.minimum(wide - wide_row, 0.0))
    lower = jnp.where(strict, beta * ratio * kk, 0.0)
    attend = jnp.where(incl, ratio * qk, 0.0)
    growth = jnp.exp(wide)
    end = wide[SPAN - 1 : SPAN, :]
    tail = jnp.exp(end - wide) * rk_wide
    rhs = jnp.concatenate([beta * v, beta * growth * rk_wide * kf], axis=1)
    return dict(i=i, h=h, lower=lower, attend=attend, tail=tail, rhs=rhs, kt2=kt2, grown=growth * qn, decay=jnp.exp(end))


def main_kernel(
    arr_ref, prompt_ref, q_hbm, k_hbm, v_hbm, gate_hbm, beta_hbm, decay_hbm, gain_hbm, w_ref,
    out_ref,
    q_ref, k_ref, v_ref, gate_ref, beta_ref, decay_ref, gain_ref,
    m_ref, o_ref, d_ref, ql_ref, lo_ref, inv_vmem, inv_ref,
    m_all, o_all, d_all, stream, states, entry, normed, rows_all, w_all, part, got,
    in_sem, inv_sem, w_send, w_recv, w_local, c_send, c_recv, m_send, m_recv, o_send, o_recv, d_send, d_recv,
    s_send, s_recv, n_send, n_recv, r_send, r_recv, p_send, p_recv,
):
    ctx = lax.axis_index("ctx")
    head = lax.axis_index("head")
    chip, core = lax.div(ctx, 2), lax.rem(ctx, 2)
    sibling = 2 * chip + 1 - core
    side_x, side_y = lax.div(head, SIDE), lax.rem(head, SIDE)

    def ctx_peer(k):
        return lax.rem(ctx + k, PEERS)

    def y_peer(k):
        return side_x * SIDE + lax.rem(side_y + k, SIDE)

    def x_peer(k):
        return lax.rem(side_x + k, SIDE) * SIDE + side_y

    barrier = pltpu.get_barrier_semaphore()

    def greet(k, carry):
        pl.semaphore_signal(barrier, inc=1, device_id=(ctx_peer(k), head), device_id_type=MESH)
        return carry

    loads = [
        pltpu.make_async_copy(src, dst, in_sem.at[n])
        for n, (src, dst) in enumerate(
            (
                (k_hbm, k_ref), (q_hbm, q_ref), (beta_hbm, beta_ref), (decay_hbm, decay_ref),
                (v_hbm, v_ref), (gate_hbm, gate_ref), (gain_hbm, gain_ref),
            )
        )
    ]
    for load in loads:
        load.start()
    lax.fori_loop(1, PEERS, greet, 0)
    for k in range(1, SIDE):
        pl.semaphore_signal(barrier, inc=1, device_id=(ctx, y_peer(k)), device_id_type=MESH)
        pl.semaphore_signal(barrier, inc=1, device_id=(ctx, x_peer(k)), device_id_type=MESH)

    def remote(src, dst, send, recv, target):
        return pltpu.make_async_remote_copy(
            src_ref=src, dst_ref=dst, send_sem=send, recv_sem=recv, device_id=target, device_id_type=MESH
        )

    def o_copy(k):
        to = ctx_peer(k)
        return remote(
            o_ref.at[lax.rem(to, 2), lax.div(to, 2)], o_all.at[pl.ds(LOCAL * ctx, LOCAL)],
            o_send.at[k], o_recv.at[k], (to, head),
        )

    def d_copy(k):
        return remote(
            d_ref, d_all.at[pl.ds(pl.multiple_of(8 * ctx, 8), 8)],
            d_send.at[k], d_recv.at[k], (ctx_peer(k), head),
        )

    def m_slot(source, g):
        return m_all.at[pl.ds(LOCAL * source + GROUP * g, GROUP)]

    def m_near(z):
        return lax.rem(chip + z + CHIPS, CHIPS)

    def m_first(h, step, g, n):
        return remote(
            m_ref.at[h, pl.ds(GROUP * g, GROUP)], m_slot(ctx, g), m_send.at[n], m_recv.at[2 * ctx + g],
            (2 * m_near(step) + h, head),
        )

    def m_sibling(g, n):
        return remote(
            m_ref.at[1 - core, pl.ds(GROUP * g, GROUP)], m_slot(ctx, g), m_send.at[n], m_recv.at[2 * ctx + g],
            (sibling, head),
        )

    def m_next(source, g, step, n):
        return remote(
            m_slot(source, g), m_slot(source, g), m_send.at[n], m_recv.at[2 * source + g],
            (2 * m_near(step) + core, head),
        )

    def w_half(half):
        return w_ref.at[:, pl.ds(pl.multiple_of(half * (MODEL // 2), MODEL // 2), MODEL // 2)]

    def pick(over_x, over_y):
        return core * over_x + (1 - core) * over_y

    def w_copy(k):
        to = pick(x_peer(k), y_peer(k))
        return remote(w_half(core), w_all.at[core, pick(side_x, side_y)], w_send.at[k], w_recv.at[k], (ctx, to))

    def w_pass(k):
        slot = w_all.at[core, lax.rem(pick(side_x, side_y) + k, SIDE)]
        return remote(slot, slot, c_send.at[k], c_recv.at[k], (sibling, head))

    row = lax.broadcasted_iota(jnp.int32, (SPAN, SPAN), 0)
    col = lax.broadcasted_iota(jnp.int32, (SPAN, SPAN), 1)
    differ = row ^ col
    incl = row >= col
    strict = row > col
    tri = incl.astype(F32).astype(BF16)
    masks = [((differ >= s) & (differ < 2 * s)).astype(F32).astype(BF16) for s in (2, 4, 8, 16, 32, 64)]
    first = (differ == 1).astype(F32)
    eye = (row == col).astype(F32)
    sent = []
    everything = []

    for load in loads[:5]:
        load.wait()
    for g in range(LOCAL // GROUP):
        chains = []
        for i in range(g * GROUP, (g + 1) * GROUP):
            rows = pl.ds(i * SPAN, SPAN)
            q = q_ref[rows, :]
            k = k_ref[rows, :]
            qf = q.astype(F32)
            kf = k.astype(F32)
            rq = lax.rsqrt(jnp.sum(qf * qf, axis=-1, keepdims=True) + 1e-6) * DK**-0.5
            rk = lax.rsqrt(jnp.sum(kf * kf, axis=-1, keepdims=True) + 1e-6)
            rk_wide = spread_lanes(rk)
            rk_row = rk_wide.T
            both = mm_t(jnp.concatenate([k, q], axis=0), k)
            kk = both[:SPAN] * rk_wide * rk_row
            qk = both[SPAN:] * spread_lanes(rq) * rk_row
            kt = k.T
            shared = (qf * rq, kf, jnp.concatenate([kt, kt], axis=1), rk_wide, kk, qk)
            logits = beta_ref[:, rows].astype(F32)
            decays = decay_ref[:, rows].astype(F32)
            for h in range(HEADS):
                chains.append(
                    block_terms(
                        i, h, q, k, logits[h : h + 1], decays[h : h + 1],
                        v_ref[rows, h * DV : (h + 1) * DV].astype(F32), shared, (tri, strict, incl),
                    )
                )
        for c in chains:
            c["parts"] = split(c["lower"])
            c["inverse"] = eye - c["lower"] * first
        for mask in masks:
            for c in chains:
                c["halves"] = split(c["inverse"])
                off = (c["parts"][0] * mask, c["parts"][1] * mask)
                c["inner"] = product(off, c["halves"])
            for c in chains:
                c["inverse"] = c["inverse"] - product(c["halves"], split(c["inner"]))
        for c in chains:
            c["solved"] = product(split(c["inverse"]), split(c["rhs"]))
        for c in chains:
            tail2 = jnp.concatenate([c["tail"], c["tail"]], axis=1)
            high, low = split(tail2 * c["solved"])
            shift = mm(c["kt2"], jnp.concatenate([high, low], axis=0))
            i, h = c["i"], c["h"]
            m_ref[h, i] = shift[:, DV:].T.astype(BF16)
            o_ref[h, :, i] = shift[:, :DV].T.reshape(CHIPS, SLICE, DK).astype(BF16)
            d_ref[h * LOCAL + i : h * LOCAL + i + 1, :] = c["decay"]
        everything += chains
        if g == 0:
            pl.semaphore_wait(barrier, PEERS - 1 + 2 * (SIDE - 1))
        firsts = [m_first(h, step, g, g * 5 + n) for n, (h, step) in enumerate(((0, 1), (0, -1), (1, 1), (1, -1)))]
        firsts.append(m_sibling(g, g * 5 + 4))
        for copy in firsts:
            copy.start()
        sent += firsts
        if g == 0:
            for k in range(1, SIDE):
                copy = w_copy(k)
                copy.start()
                sent.append(copy)
            w_own = [
                pltpu.make_async_copy(w_half(half), w_all.at[half, side], w_local.at[half])
                for half, side in enumerate((side_y, side_x))
            ]
            for copy in w_own:
                copy.start()

    def send_small(k, carry):
        d_copy(k).start()
        o_copy(k).start()
        return carry

    lax.fori_loop(1, PEERS, send_small, 0)
    m_all[pl.ds(LOCAL * ctx, LOCAL)] = m_ref[core]
    o_all[pl.ds(LOCAL * ctx, LOCAL)] = o_ref[core, chip]
    d_all[pl.ds(pl.multiple_of(8 * ctx, 8), 8), :] = d_ref[...]

    lanes = lax.broadcasted_iota(jnp.int32, (1, SPAN), 1)
    found = jnp.zeros((1, SPAN), jnp.int32)
    for t in range(BLOCKS):
        found = jnp.where(lanes == arr_ref[t], t, found)
    inv_vmem[...] = found
    inv_copy = pltpu.make_async_copy(inv_vmem, inv_ref, inv_sem)
    inv_copy.start()
    bits = jnp.int32(0)
    start = prompt_ref[0]
    for i in range(1, 7):
        bits = bits | (jnp.int32(1) << start)
        start = start + prompt_ref[i]

    for c in everything:
        i, h = c["i"], c["h"]
        local = product(split(c["attend"]), split(c["solved"]))
        lo_ref[h, i] = local[:, :DV]
        ql_ref[h, i] = c["grown"] - local[:, DV:]

    n = 10
    for k in range(1, 5):
        for g in range(LOCAL // GROUP):
            for step in (1, -1):
                for s in range(2):
                    last = 4 if (s == 0) == (step == 1) else 3
                    if k > last:
                        continue
                    source = 2 * m_near(-step * k) + s
                    m_next(source, g, step, 0).wait_recv()
                    if k < last:
                        copy = m_next(source, g, step, n)
                        copy.start()
                        sent.append(copy)
                        n += 1
    for g in range(LOCAL // GROUP):
        m_next(sibling, g, 0, 0).wait_recv()

    def wait_small(k, carry):
        d_copy(k).wait()
        o_copy(k).wait()
        return carry

    lax.fori_loop(1, PEERS, wait_small, 0)
    inv_copy.wait()

    def advance(state, t):
        slot = arr_ref[t]
        stream[t] = state.astype(BF16)
        high, low = split(state)
        moved = mm(jnp.concatenate([high, low], axis=0), m_all[slot])
        decay = d_all[pl.ds(lax.div(slot, LOCAL) * 8 + core * LOCAL + lax.rem(slot, LOCAL), 1), :]
        return decay * state - moved[:SLICE] - moved[SLICE:] + o_all[slot].astype(F32)

    def step(t, pair):
        keep = (1 - ((bits >> t) & 1)).astype(F32)
        return advance(keep * pair[0], t), advance(pair[1], t + CHAIN)

    empty = jnp.zeros((SLICE, DK), F32)
    lax.fori_loop(0, CHAIN, step, (empty, empty), unroll=4)

    def place(a, carry):
        states[a] = stream[inv_ref[0, a]]
        return carry

    lax.fori_loop(0, BLOCKS, place, 0, unroll=8)

    def s_rows(h, z):
        return entry.at[h, :, pl.ds(pl.multiple_of(SLICE * z, SLICE), SLICE), :]

    def s_copy(k):
        to = ctx_peer(k)
        return remote(
            states.at[pl.ds(LOCAL * to, LOCAL)], s_rows(core, chip), s_send.at[k], s_recv.at[k], (to, head)
        )

    def s_arrival(k):
        source = lax.rem(ctx - k + PEERS, PEERS)
        return remote(
            states.at[pl.ds(0, LOCAL)], s_rows(lax.rem(source, 2), lax.div(source, 2)),
            s_send.at[k], s_recv.at[k], (ctx, head),
        )

    def send_states(k, carry):
        s_copy(k).start()
        return carry

    lax.fori_loop(1, PEERS, send_states, 0)
    entry[core, :, pl.ds(pl.multiple_of(SLICE * chip, SLICE), SLICE), :] = states[pl.ds(LOCAL * ctx, LOCAL)]
    for copy in w_own:
        copy.wait()
    for k in range(1, SIDE):
        w_copy(SIDE - k).wait_recv()
        copy = w_pass(k)
        copy.start()
        sent.append(copy)
    for load in loads[5:]:
        load.wait()

    def wait_states(k, carry):
        s_copy(k).wait_send()
        s_arrival(k).wait_recv()
        return carry

    lax.fori_loop(1, PEERS, wait_states, 0)

    def n_copy(i, k):
        return remote(
            normed.at[i, lax.rem(side_y + k, SIDE)], rows_all.at[0, side_y, i],
            n_send.at[i * SIDE + k], n_recv.at[i * SIDE + k], (ctx, y_peer(k)),
        )

    def r_copy(i):
        return remote(
            normed.at[i], rows_all.at[1, side_x], r_send.at[i], r_recv.at[side_x], (ctx, i * SIDE + side_y)
        )

    def r_arrival(x):
        return remote(normed.at[x], rows_all.at[1, x], r_send.at[x], r_recv.at[x], (ctx, head))

    gain = gain_ref[...]
    for i in range(LOCAL):
        for h in range(HEADS):
            high, low = split(ql_ref[h, i])
            state = entry[h, i]
            both = mm_t(jnp.concatenate([high, low], axis=0), state)
            core_out = both[:SPAN] + both[SPAN:] + lo_ref[h, i]
            scale = lax.rsqrt(jnp.mean(core_out * core_out, axis=-1, keepdims=True) + 1e-6)
            gate = gate_ref[i * SPAN : (i + 1) * SPAN, h * DV : (h + 1) * DV].astype(F32)
            value = core_out * scale * gain * (gate / (1.0 + jnp.exp(-gate)))
            normed[i, :, :, h * DV : (h + 1) * DV] = value.astype(BF16).reshape(SIDE, 32, DV)
        for k in range(1, SIDE):
            copy = n_copy(i, k)
            copy.start()
            sent.append(copy)

        @pl.when(i != side_x)
        def _():
            r_copy(i).start()

    rows_all[0, side_y] = normed[:, side_y]
    rows_all[1, side_x] = normed[side_x]
    for k in range(1, SIDE):
        w_pass(k).wait_recv()
    for i in range(LOCAL):
        for k in range(1, SIDE):
            n_copy(i, k).wait_recv()

    def p_copy(piece, k):
        if piece < PIECES // 2:
            source, to = lax.rem(side_x + k, SIDE), x_peer(k)
        else:
            source, to = lax.rem(side_y + k, SIDE), y_peer(k)
        return remote(
            part.at[piece, source], got.at[piece, k],
            p_send.at[piece * SIDE + k], p_recv.at[piece * SIDE + k], (ctx, to),
        )

    for piece in range(PIECES):
        half, off = divmod(piece * PIECE, MODEL // 2)
        if piece == PIECES // 2:
            for x in range(SIDE):

                @pl.when(x != side_x)
                def _():
                    r_arrival(x).wait_recv()

        if off == 0:
            left = jnp.concatenate(
                [rows_all[half, n].reshape(SPAN, HEADS * DV) for n in range(SIDE)], axis=1
            )
        right = w_all[half, :, :, off : off + PIECE].reshape(SIDE * HEADS * DV, PIECE)
        total = mm(left, right)
        part[piece] = total.astype(BF16).reshape(SIDE, 32, PIECE)
        for k in range(1, SIDE):
            copy = p_copy(piece, k)
            copy.start()
            sent.append(copy)
    for piece in range(PIECES):
        total = part[piece, side_x if piece < PIECES // 2 else side_y].astype(F32)
        for k in range(1, SIDE):
            p_copy(piece, k).wait_recv()
            total = total + got[piece, k].astype(F32)
        out_ref[:, piece * PIECE : (piece + 1) * PIECE] = total.astype(BF16)
    for i in range(LOCAL):

        @pl.when(i != side_x)
        def _():
            r_copy(i).wait_send()

    for copy in sent:
        copy.wait_send()


def per_device(q_rows, k_rows, v_rows, gate_rows, beta_logits, log_decay, norm_gain, out_weight, prompt_blocks, arrival_slot):
    smem = pl.BlockSpec(memory_space=pltpu.SMEM)
    vmem = pl.BlockSpec(memory_space=pltpu.VMEM)
    whole = pl.BlockSpec(memory_space=pl.ANY)
    tokens = LOCAL * SPAN
    dma = pltpu.SemaphoreType.DMA
    return pl.pallas_call(
        main_kernel,
        out_shape=pltpu.VMEM((tokens // PEERS, MODEL), BF16),
        in_specs=[smem, smem] + [whole] * 8,
        out_specs=vmem,
        scratch_shapes=[
            pltpu.VMEM((tokens, DK), BF16),
            pltpu.VMEM((tokens, DK), BF16),
            pltpu.VMEM((tokens, HEADS * DV), BF16),
            pltpu.VMEM((tokens, HEADS * DV), BF16),
            pltpu.VMEM((HEADS, tokens), BF16),
            pltpu.VMEM((HEADS, tokens), BF16),
            pltpu.VMEM((1, DV), F32),
            pltpu.VMEM((HEADS, LOCAL, DK, DK), BF16),
            pltpu.VMEM((HEADS, CHIPS, LOCAL, SLICE, DK), BF16),
            pltpu.VMEM((HEADS * LOCAL, DK), F32),
            pltpu.VMEM((HEADS, LOCAL, SPAN, DK), F32),
            pltpu.VMEM((HEADS, LOCAL, SPAN, DV), F32),
            pltpu.VMEM((1, SPAN), jnp.int32),
            pltpu.SMEM((1, SPAN), jnp.int32),
            pltpu.VMEM((BLOCKS, DK, DK), BF16),
            pltpu.VMEM((BLOCKS, SLICE, DK), BF16),
            pltpu.VMEM((PEERS * HEADS * LOCAL, DK), F32),
            pltpu.VMEM((BLOCKS, SLICE, DK), BF16),
            pltpu.VMEM((BLOCKS, SLICE, DK), BF16),
            pltpu.VMEM((HEADS, LOCAL, DV, DK), BF16),
            pltpu.VMEM((LOCAL, SIDE, 32, HEADS * DV), BF16),
            pltpu.VMEM((2, SIDE, LOCAL, 32, HEADS * DV), BF16),
            pltpu.VMEM((2, SIDE, HEADS * DV, MODEL // 2), BF16),
            pltpu.VMEM((PIECES, SIDE, 32, PIECE), BF16),
            pltpu.VMEM((PIECES, SIDE, 32, PIECE), BF16),
            dma((7,)), dma, dma((SIDE,)), dma((SIDE,)), dma((2,)), dma((SIDE,)), dma((SIDE,)),
            dma((30,)), dma((2 * PEERS,)),
            dma((PEERS,)), dma((PEERS,)), dma((PEERS,)), dma((PEERS,)),
            dma((PEERS,)), dma((PEERS,)), dma((LOCAL * SIDE,)), dma((LOCAL * SIDE,)), dma((SIDE,)), dma((SIDE,)),
            dma((PIECES * SIDE,)), dma((PIECES * SIDE,)),
        ],
        compiler_params=pltpu.CompilerParams(
            collective_id=0, has_side_effects=True, vmem_limit_bytes=VMEM_LIMIT
        ),
    )(
        arrival_slot, prompt_blocks, q_rows, k_rows, v_rows, gate_rows, beta_logits.T, log_decay.T,
        norm_gain.reshape(1, DV), out_weight,
    )


def solution(mesh):
    in_specs = (
        P("ctx", "head"),
        P("ctx", "head"),
        P("ctx", "head"),
        P("ctx", "head"),
        P("ctx", "head"),
        P("ctx", "head"),
        P(),
        P("head", None),
        P(),
        P(),
    )
    return jax.shard_map(
        per_device, mesh=mesh, in_specs=in_specs, out_specs=P(("ctx", "head"), None), check_vma=False
    )
```

```python
import jax
import jax.numpy as jnp
from jax import lax
from jax.experimental import pallas as pl
from jax.experimental.pallas import tpu as pltpu
from jax.sharding import PartitionSpec as P

SPAN = 128
DK = 128
DV = 128
HEADS = 2
LOCAL = 4
PEERS = 16
CHIPS = 8
SLICE = 16
BLOCKS = 64
CHAIN = 32
SIDE = 4
MODEL = 2048
PIECES = 4
PIECE = MODEL // PIECES
GROUP = 2
VMEM_LIMIT = 60 * 2**20
MESH = pl.DeviceIdType.MESH
F32 = jnp.float32
BF16 = jnp.bfloat16


def split(x):
    high = x.astype(BF16)
    return high, (x - high.astype(F32)).astype(BF16)


def mm(a, b):
    return jnp.dot(a, b, preferred_element_type=F32)


def mm_t(a, b):
    return lax.dot_general(a, b, (((1,), (1,)), ((), ())), preferred_element_type=F32)


def product(a, b):
    a_high, a_low = a
    b_high, b_low = b
    n = b_high.shape[1]
    if n == 128:
        left = jnp.concatenate([a_high, a_low], axis=1)
        right = jnp.concatenate(
            [
                jnp.concatenate([b_high, b_low], axis=1),
                jnp.concatenate([b_high, jnp.zeros_like(b_low)], axis=1),
            ],
            axis=0,
        )
        both = mm(left, right)
        return both[:, :n] + both[:, n:]
    left = jnp.concatenate([a_high, a_low], axis=1)
    right = jnp.concatenate([b_high, b_high], axis=0)
    return mm(left, right) + mm(a_high, b_low)


def spread_lanes(column):
    return jnp.broadcast_to(column, (column.shape[0], 128))


def block_terms(i, h, q, k, beta_row, decay_row, v, shared, consts):
    tri, strict, incl = consts
    qn, kf, kt2, rk_wide, kk, qk = shared
    beta = jnp.broadcast_to(1.0 / (1.0 + jnp.exp(-beta_row)), (SPAN, SPAN)).T
    steps = jnp.broadcast_to(decay_row, (SPAN, SPAN)).astype(BF16)
    wide = mm_t(tri, steps)
    wide_row = mm_t(steps, tri)
    ratio = jnp.exp(jnp.minimum(wide - wide_row, 0.0))
    lower = jnp.where(strict, beta * ratio * kk, 0.0)
    attend = jnp.where(incl, ratio * qk, 0.0)
    growth = jnp.exp(wide)
    end = wide[SPAN - 1 : SPAN, :]
    tail = jnp.exp(end - wide) * rk_wide
    rhs = jnp.concatenate([beta * v, beta * growth * rk_wide * kf], axis=1)
    return dict(i=i, h=h, lower=lower, attend=attend, tail=tail, rhs=rhs, kt2=kt2, grown=growth * qn, decay=jnp.exp(end))


def main_kernel(
    arr_ref, prompt_ref, q_hbm, k_hbm, v_hbm, gate_hbm, beta_hbm, decay_hbm, gain_hbm, w_ref,
    out_ref,
    q_ref, k_ref, v_ref, gate_ref, beta_ref, decay_ref, gain_ref,
    m_ref, o_ref, d_ref, ql_ref, lo_ref, inv_vmem, inv_ref,
    m_all, o_all, d_all, stream, states, entry, normed, rows_all, w_all, part, got,
    in_sem, inv_sem, w_send, w_recv, w_local, c_send, c_recv, m_send, m_recv, o_send, o_recv,
    s_send, s_recv, n_send, n_recv, r_send, r_recv, p_send, p_recv,
):
    ctx = lax.axis_index("ctx")
    head = lax.axis_index("head")
    chip, core = lax.div(ctx, 2), lax.rem(ctx, 2)
    sibling = 2 * chip + 1 - core
    side_x, side_y = lax.div(head, SIDE), lax.rem(head, SIDE)

    def ctx_peer(k):
        return lax.rem(ctx + k, PEERS)

    def y_peer(k):
        return side_x * SIDE + lax.rem(side_y + k, SIDE)

    def x_peer(k):
        return lax.rem(side_x + k, SIDE) * SIDE + side_y

    barrier = pltpu.get_barrier_semaphore()

    loads = [
        pltpu.make_async_copy(src, dst, in_sem.at[n])
        for n, (src, dst) in enumerate(
            (
                (k_hbm, k_ref), (q_hbm, q_ref), (beta_hbm, beta_ref), (decay_hbm, decay_ref),
                (v_hbm, v_ref), (gate_hbm, gate_ref), (gain_hbm, gain_ref),
            )
        )
    ]
    for load in loads:
        load.start()
    for k in range(1, PEERS):
        pl.semaphore_signal(barrier, inc=1, device_id=(ctx_peer(k), head), device_id_type=MESH)
    for k in range(1, SIDE):
        pl.semaphore_signal(barrier, inc=1, device_id=(ctx, y_peer(k)), device_id_type=MESH)
        pl.semaphore_signal(barrier, inc=1, device_id=(ctx, x_peer(k)), device_id_type=MESH)

    def remote(src, dst, send, recv, target):
        return pltpu.make_async_remote_copy(
            src_ref=src, dst_ref=dst, send_sem=send, recv_sem=recv, device_id=target, device_id_type=MESH
        )

    def finish_sends(ref, sem):
        remote(ref, ref, sem, sem, (ctx, head)).wait_send()

    def finish_arrivals(ref, sem):
        remote(ref, ref, sem, sem, (ctx, head)).wait_recv()

    def o_copy(k):
        to = ctx_peer(k)
        return remote(o_ref.at[lax.rem(to, 2), lax.div(to, 2)], o_all.at[ctx], o_send, o_recv, (to, head))

    def m_slot(source, g):
        return m_all.at[pl.ds(LOCAL * source + GROUP * g, GROUP)]

    def m_near(z):
        return lax.rem(chip + z + CHIPS, CHIPS)

    def m_first(h, step, g):
        return remote(
            m_ref.at[h, pl.ds(GROUP * g, GROUP)], m_slot(ctx, g), m_send, m_recv.at[2 * ctx + g],
            (2 * m_near(step) + h, head),
        )

    def m_sibling(g):
        return remote(
            m_ref.at[1 - core, pl.ds(GROUP * g, GROUP)], m_slot(ctx, g), m_send, m_recv.at[2 * ctx + g],
            (sibling, head),
        )

    def m_next(source, g, step):
        return remote(
            m_slot(source, g), m_slot(source, g), m_send, m_recv.at[2 * source + g],
            (2 * m_near(step) + core, head),
        )

    def forward(k, g):
        for step in (1, -1):
            for s in range(2):
                last = 4 if (s == 0) == (step == 1) else 3
                if k > last:
                    continue
                source = 2 * m_near(-step * k) + s
                m_next(source, g, step).wait_recv()
                if k < last:
                    m_next(source, g, step).start()

    def attend_locally(chains):
        for c in chains:
            i, h = c["i"], c["h"]
            local = product(split(c["attend"]), split(c["solved"]))
            lo_ref[h, i] = local[:, :DV]
            ql_ref[h, i] = c["grown"] - local[:, DV:]

    def w_half(half):
        return w_ref.at[:, pl.ds(pl.multiple_of(half * (MODEL // 2), MODEL // 2), MODEL // 2)]

    def pick(over_x, over_y):
        return core * over_x + (1 - core) * over_y

    def w_copy(k):
        to = pick(x_peer(k), y_peer(k))
        return remote(w_half(core), w_all.at[core, pick(side_x, side_y)], w_send, w_recv, (ctx, to))

    def w_pass(k):
        slot = w_all.at[core, lax.rem(pick(side_x, side_y) + k, SIDE)]
        return remote(slot, slot, c_send, c_recv, (sibling, head))

    row = lax.broadcasted_iota(jnp.int32, (SPAN, SPAN), 0)
    col = lax.broadcasted_iota(jnp.int32, (SPAN, SPAN), 1)
    differ = row ^ col
    incl = row >= col
    strict = row > col
    tri = incl.astype(F32).astype(BF16)
    masks = [((differ >= s) & (differ < 2 * s)).astype(F32).astype(BF16) for s in (2, 4, 8, 16, 32, 64)]
    first = (differ == 1).astype(F32)
    eye = (row == col).astype(F32)
    d_ref[...] = jnp.zeros((HEADS, SLICE, DK), F32)
    everything = []

    for load in loads[:5]:
        load.wait()
    for g in range(LOCAL // GROUP):
        chains = []
        for i in range(g * GROUP, (g + 1) * GROUP):
            rows = pl.ds(i * SPAN, SPAN)
            q = q_ref[rows, :]
            k = k_ref[rows, :]
            qf = q.astype(F32)
            kf = k.astype(F32)
            rq = lax.rsqrt(jnp.sum(qf * qf, axis=-1, keepdims=True) + 1e-6) * DK**-0.5
            rk = lax.rsqrt(jnp.sum(kf * kf, axis=-1, keepdims=True) + 1e-6)
            rk_wide = spread_lanes(rk)
            rk_row = rk_wide.T
            both = mm_t(jnp.concatenate([k, q], axis=0), k)
            kk = both[:SPAN] * rk_wide * rk_row
            qk = both[SPAN:] * spread_lanes(rq) * rk_row
            kt = k.T
            shared = (qf * rq, kf, jnp.concatenate([kt, kt], axis=1), rk_wide, kk, qk)
            logits = beta_ref[:, rows].astype(F32)
            decays = decay_ref[:, rows].astype(F32)
            for h in range(HEADS):
                chains.append(
                    block_terms(
                        i, h, q, k, logits[h : h + 1], decays[h : h + 1],
                        v_ref[rows, h * DV : (h + 1) * DV].astype(F32), shared, (tri, strict, incl),
                    )
                )
        for c in chains:
            c["parts"] = split(c["lower"])
            c["inverse"] = eye - c["lower"] * first
        for mask in masks:
            for c in chains:
                c["halves"] = split(c["inverse"])
                off = (c["parts"][0] * mask, c["parts"][1] * mask)
                c["inner"] = product(off, c["halves"])
            for c in chains:
                c["inverse"] = c["inverse"] - product(c["halves"], split(c["inner"]))
        for c in chains:
            c["solved"] = product(split(c["inverse"]), split(c["rhs"]))
        for c in chains:
            tail2 = jnp.concatenate([c["tail"], c["tail"]], axis=1)
            high, low = split(tail2 * c["solved"])
            shift = mm(c["kt2"], jnp.concatenate([high, low], axis=0))
            i, h = c["i"], c["h"]
            m_ref[h, i] = shift[:, DV:].T.astype(BF16)
            o_ref[h, :, i] = shift[:, :DV].T.reshape(CHIPS, SLICE, DK).astype(BF16)
            decay = c["decay"].astype(BF16).astype(F32)
            d_ref[h, i : i + 1, :] = decay
            d_ref[h, 8 + i : 9 + i, :] = c["decay"] - decay
        everything += chains
        if g == 0:
            pl.semaphore_wait(barrier, PEERS - 1 + 2 * (SIDE - 1))
        for h, step in ((0, 1), (0, -1), (1, 1), (1, -1)):
            m_first(h, step, g).start()
        m_sibling(g).start()
        if g == 0:
            for k in range(1, SIDE):
                w_copy(k).start()
            w_own = [
                pltpu.make_async_copy(w_half(half), w_all.at[half, side], w_local.at[half])
                for half, side in enumerate((side_y, side_x))
            ]
            for copy in w_own:
                copy.start()

    forward(1, 0)
    for h in range(HEADS):
        o_ref[h, :, LOCAL] = jnp.broadcast_to(d_ref[h].astype(BF16), (CHIPS, SLICE, DK))
    for k in range(1, PEERS):
        o_copy(k).start()
    m_all[pl.ds(LOCAL * ctx, LOCAL)] = m_ref[core]
    o_all[ctx] = o_ref[core, chip]
    forward(1, 1)
    attend_locally(everything[: len(everything) // 2])
    forward(2, 0)
    attend_locally(everything[len(everything) // 2 :])
    forward(2, 1)

    lanes = lax.broadcasted_iota(jnp.int32, (1, SPAN), 1)
    found = jnp.zeros((1, SPAN), jnp.int32)
    for t in range(BLOCKS):
        found = jnp.where(lanes == arr_ref[t], t, found)
    inv_vmem[...] = found
    inv_copy = pltpu.make_async_copy(inv_vmem, inv_ref, inv_sem)
    inv_copy.start()
    bits = jnp.int32(0)
    start = prompt_ref[0]
    for i in range(1, 7):
        bits = bits | (jnp.int32(1) << start)
        start = start + prompt_ref[i]

    for k in (3, 4):
        for g in range(LOCAL // GROUP):
            forward(k, g)
    for g in range(LOCAL // GROUP):
        m_next(sibling, g, 0).wait_recv()
    finish_arrivals(o_all.at[pl.ds(0, PEERS - 1)], o_recv)
    for source in range(PEERS):
        tile = o_all[source, LOCAL].astype(F32)
        d_all[source * 8 : source * 8 + 8, :] = tile[:8] + tile[8:]
    inv_copy.wait()

    def advance(state, t):
        slot = arr_ref[t]
        stream[t] = state.astype(BF16)
        high, low = split(state)
        moved = mm(jnp.concatenate([high, low], axis=0), m_all[slot])
        source, i = lax.div(slot, LOCAL), lax.rem(slot, LOCAL)
        decay = d_all[pl.ds(source * 8 + i, 1), :]
        return decay * state + o_all[source, i].astype(F32) - (moved[:SLICE] + moved[SLICE:])

    def step(t, pair):
        keep = (1 - ((bits >> t) & 1)).astype(F32)
        return advance(keep * pair[0], t), advance(pair[1], t + CHAIN)

    empty = jnp.zeros((SLICE, DK), F32)
    lax.fori_loop(0, CHAIN, step, (empty, empty), unroll=16)

    def place(a, carry):
        states[a] = stream[inv_ref[0, a]]
        return carry

    lax.fori_loop(0, BLOCKS, place, 0, unroll=8)

    def s_rows(h, z):
        return entry.at[h, :, pl.ds(pl.multiple_of(SLICE * z, SLICE), SLICE), :]

    def s_copy(k):
        to = ctx_peer(k)
        return remote(states.at[pl.ds(LOCAL * to, LOCAL)], s_rows(core, chip), s_send, s_recv, (to, head))

    for k in range(1, PEERS):
        s_copy(k).start()
    entry[core, :, pl.ds(pl.multiple_of(SLICE * chip, SLICE), SLICE), :] = states[pl.ds(LOCAL * ctx, LOCAL)]
    for copy in w_own:
        copy.wait()
    finish_arrivals(w_all.at[0, pl.ds(0, SIDE - 1)], w_recv)
    for k in range(1, SIDE):
        w_pass(k).start()
    for load in loads[5:]:
        load.wait()
    finish_arrivals(states.at[pl.ds(0, LOCAL * (PEERS - 1))], s_recv)

    def n_copy(k):
        return remote(
            normed.at[:, lax.rem(side_y + k, SIDE)], rows_all.at[0, side_y], n_send, n_recv, (ctx, y_peer(k))
        )

    def r_copy(i):
        return remote(normed.at[i], rows_all.at[1, side_x], r_send, r_recv, (ctx, i * SIDE + side_y))

    gain = gain_ref[...]
    for i in range(LOCAL):
        for h in range(HEADS):
            high, low = split(ql_ref[h, i])
            state = entry[h, i]
            both = mm_t(jnp.concatenate([high, low], axis=0), state)
            core_out = both[:SPAN] + both[SPAN:] + lo_ref[h, i]
            scale = lax.rsqrt(jnp.mean(core_out * core_out, axis=-1, keepdims=True) + 1e-6)
            gate = gate_ref[i * SPAN : (i + 1) * SPAN, h * DV : (h + 1) * DV].astype(F32)
            value = core_out * scale * gain * (gate / (1.0 + jnp.exp(-gate)))
            normed[i, :, :, h * DV : (h + 1) * DV] = value.astype(BF16).reshape(SIDE, 32, DV)

        @pl.when(i != side_x)
        def _():
            r_copy(i).start()

    for k in range(1, SIDE):
        n_copy(k).start()
    rows_all[0, side_y] = normed[:, side_y]
    rows_all[1, side_x] = normed[side_x]
    finish_arrivals(w_all.at[0, pl.ds(0, SIDE - 1)], c_recv)
    finish_arrivals(rows_all.at[0, pl.ds(0, SIDE - 1)], n_recv)

    def p_copy(piece, k):
        if piece < PIECES // 2:
            source, to = lax.rem(side_x + k, SIDE), x_peer(k)
        else:
            source, to = lax.rem(side_y + k, SIDE), y_peer(k)
        return remote(
            part.at[piece, source], got.at[piece, k],
            p_send, p_recv.at[piece], (ctx, to),
        )

    for piece in range(PIECES):
        half, off = divmod(piece * PIECE, MODEL // 2)
        if piece == PIECES // 2:
            finish_arrivals(rows_all.at[1, pl.ds(0, SIDE - 1)], r_recv)
        if off == 0:
            left = jnp.concatenate(
                [rows_all[half, n].reshape(SPAN, HEADS * DV) for n in range(SIDE)], axis=1
            )
        right = w_all[half, :, :, off : off + PIECE].reshape(SIDE * HEADS * DV, PIECE)
        total = mm(left, right)
        part[piece] = total.astype(BF16).reshape(SIDE, 32, PIECE)
        for k in range(1, SIDE):
            p_copy(piece, k).start()
    for piece in range(PIECES):
        total = part[piece, side_x if piece < PIECES // 2 else side_y].astype(F32)
        finish_arrivals(got.at[piece, pl.ds(1, SIDE - 1)], p_recv.at[piece])
        for k in range(1, SIDE):
            total = total + got[piece, k].astype(F32)
        out_ref[:, piece * PIECE : (piece + 1) * PIECE] = total.astype(BF16)
    finish_sends(m_all.at[pl.ds(0, LOCAL * (PEERS - 1))], m_send)
    finish_sends(o_all.at[pl.ds(0, PEERS - 1)], o_send)
    finish_sends(states.at[pl.ds(0, LOCAL * (PEERS - 1))], s_send)
    finish_sends(w_all.at[0, pl.ds(0, SIDE - 1)], w_send)
    finish_sends(w_all.at[0, pl.ds(0, SIDE - 1)], c_send)
    finish_sends(rows_all.at[0, pl.ds(0, SIDE - 1)], n_send)
    finish_sends(rows_all.at[1, pl.ds(0, SIDE - 1)], r_send)
    finish_sends(part.at[pl.ds(0, PIECES - 1)], p_send)


def per_device(q_rows, k_rows, v_rows, gate_rows, beta_logits, log_decay, norm_gain, out_weight, prompt_blocks, arrival_slot):
    smem = pl.BlockSpec(memory_space=pltpu.SMEM)
    vmem = pl.BlockSpec(memory_space=pltpu.VMEM)
    whole = pl.BlockSpec(memory_space=pl.ANY)
    tokens = LOCAL * SPAN
    dma = pltpu.SemaphoreType.DMA
    return pl.pallas_call(
        main_kernel,
        out_shape=pltpu.VMEM((tokens // PEERS, MODEL), BF16),
        in_specs=[smem, smem] + [whole] * 8,
        out_specs=vmem,
        scratch_shapes=[
            pltpu.VMEM((tokens, DK), BF16),
            pltpu.VMEM((tokens, DK), BF16),
            pltpu.VMEM((tokens, HEADS * DV), BF16),
            pltpu.VMEM((tokens, HEADS * DV), BF16),
            pltpu.VMEM((HEADS, tokens), BF16),
            pltpu.VMEM((HEADS, tokens), BF16),
            pltpu.VMEM((1, DV), F32),
            pltpu.VMEM((HEADS, LOCAL, DK, DK), BF16),
            pltpu.VMEM((HEADS, CHIPS, LOCAL + 1, SLICE, DK), BF16),
            pltpu.VMEM((HEADS, SLICE, DK), F32),
            pltpu.VMEM((HEADS, LOCAL, SPAN, DK), F32),
            pltpu.VMEM((HEADS, LOCAL, SPAN, DV), F32),
            pltpu.VMEM((1, SPAN), jnp.int32),
            pltpu.SMEM((1, SPAN), jnp.int32),
            pltpu.VMEM((BLOCKS, DK, DK), BF16),
            pltpu.VMEM((PEERS, LOCAL + 1, SLICE, DK), BF16),
            pltpu.VMEM((PEERS * 8, DK), F32),
            pltpu.VMEM((BLOCKS, SLICE, DK), BF16),
            pltpu.VMEM((BLOCKS, SLICE, DK), BF16),
            pltpu.VMEM((HEADS, LOCAL, DV, DK), BF16),
            pltpu.VMEM((LOCAL, SIDE, 32, HEADS * DV), BF16),
            pltpu.VMEM((2, SIDE, LOCAL, 32, HEADS * DV), BF16),
            pltpu.VMEM((2, SIDE, HEADS * DV, MODEL // 2), BF16),
            pltpu.VMEM((PIECES, SIDE, 32, PIECE), BF16),
            pltpu.VMEM((PIECES, SIDE, 32, PIECE), BF16),
            dma((7,)), dma, dma, dma, dma((2,)), dma, dma,
            dma, dma((2 * PEERS,)), dma, dma,
            dma, dma, dma, dma, dma, dma, dma, dma((PIECES,)),
        ],
        compiler_params=pltpu.CompilerParams(
            collective_id=0, has_side_effects=True, vmem_limit_bytes=VMEM_LIMIT
        ),
    )(
        arrival_slot, prompt_blocks, q_rows, k_rows, v_rows, gate_rows, beta_logits.T, log_decay.T,
        norm_gain.reshape(1, DV), out_weight,
    )


def solution(mesh):
    in_specs = (
        P("ctx", "head"),
        P("ctx", "head"),
        P("ctx", "head"),
        P("ctx", "head"),
        P("ctx", "head"),
        P("ctx", "head"),
        P(),
        P("head", None),
        P(),
        P(),
    )
    return jax.shard_map(
        per_device, mesh=mesh, in_specs=in_specs, out_specs=P(("ctx", "head"), None), check_vma=False
    )
```

```python
import jax
import jax.numpy as jnp
from jax import lax
from jax.experimental import pallas as pl
from jax.experimental.pallas import tpu as pltpu
from jax.sharding import PartitionSpec as P

SPAN = 128
DK = 128
DV = 128
HEADS = 2
LOCAL = 4
PEERS = 16
CHIPS = 8
SLICE = 32
ROOTS = 4
BLOCKS = 64
CHAIN = 32
SIDE = 4
MODEL = 2048
PIECES = 4
PIECE = MODEL // PIECES
GROUP = 2
VMEM_LIMIT = 60 * 2**20
MESH = pl.DeviceIdType.MESH
F32 = jnp.float32
BF16 = jnp.bfloat16


def split(x):
    high = x.astype(BF16)
    return high, (x - high.astype(F32)).astype(BF16)


def mm(a, b):
    return jnp.dot(a, b, preferred_element_type=F32)


def mm_t(a, b):
    return lax.dot_general(a, b, (((1,), (1,)), ((), ())), preferred_element_type=F32)


def product(a, b):
    a_high, a_low = a
    b_high, b_low = b
    n = b_high.shape[1]
    if n == 128:
        left = jnp.concatenate([a_high, a_low], axis=1)
        right = jnp.concatenate(
            [
                jnp.concatenate([b_high, b_low], axis=1),
                jnp.concatenate([b_high, jnp.zeros_like(b_low)], axis=1),
            ],
            axis=0,
        )
        both = mm(left, right)
        return both[:, :n] + both[:, n:]
    left = jnp.concatenate([a_high, a_low], axis=1)
    right = jnp.concatenate([b_high, b_high], axis=0)
    return mm(left, right) + mm(a_high, b_low)


def spread_lanes(column):
    return jnp.broadcast_to(column, (column.shape[0], 128))


def block_terms(i, h, q, k, beta_row, decay_row, v, shared, consts):
    tri, strict, incl = consts
    qn, kf, kt2, rk_wide, kk, qk = shared
    beta = jnp.broadcast_to(1.0 / (1.0 + jnp.exp(-beta_row)), (SPAN, SPAN)).T
    steps = jnp.broadcast_to(decay_row, (SPAN, SPAN)).astype(BF16)
    wide = mm_t(tri, steps)
    wide_row = mm_t(steps, tri)
    ratio = jnp.exp(jnp.minimum(wide - wide_row, 0.0))
    lower = jnp.where(strict, beta * ratio * kk, 0.0)
    attend = jnp.where(incl, ratio * qk, 0.0)
    growth = jnp.exp(wide)
    end = wide[SPAN - 1 : SPAN, :]
    tail = jnp.exp(end - wide) * rk_wide
    rhs = jnp.concatenate([beta * v, beta * growth * rk_wide * kf], axis=1)
    return dict(i=i, h=h, lower=lower, attend=attend, tail=tail, rhs=rhs, kt2=kt2, grown=growth * qn, decay=jnp.exp(end))


def main_kernel(
    arr_ref, prompt_ref, q_hbm, k_hbm, v_hbm, gate_hbm, beta_hbm, decay_hbm, gain_hbm, w_ref,
    out_ref,
    q_ref, k_ref, v_ref, gate_ref, beta_ref, decay_ref, gain_ref,
    m_ref, o_ref, d_ref, ql_ref, lo_ref, inv_vmem, inv_ref,
    m_all, o_all, d_all, stream, states, entry, normed, rows_all, w_all, part, got,
    in_sem, inv_sem, w_send, w_recv, w_local, c_send, c_recv, m_send, m_recv, m_pass, o_send, o_recv,
    s_send, s_recv, n_send, n_recv, r_send, r_recv, p_send, p_recv,
):
    ctx = lax.axis_index("ctx")
    head = lax.axis_index("head")
    chip, core = lax.div(ctx, 2), lax.rem(ctx, 2)
    sibling = 2 * chip + 1 - core
    side_x, side_y = lax.div(head, SIDE), lax.rem(head, SIDE)

    def ctx_peer(k):
        return lax.rem(ctx + k, PEERS)

    def y_peer(k):
        return side_x * SIDE + lax.rem(side_y + k, SIDE)

    def x_peer(k):
        return lax.rem(side_x + k, SIDE) * SIDE + side_y

    barrier = pltpu.get_barrier_semaphore()

    loads = [
        pltpu.make_async_copy(src, dst, in_sem.at[n])
        for n, (src, dst) in enumerate(
            (
                (k_hbm, k_ref), (q_hbm, q_ref), (beta_hbm, beta_ref), (decay_hbm, decay_ref),
                (v_hbm, v_ref), (gate_hbm, gate_ref), (gain_hbm, gain_ref),
            )
        )
    ]
    for load in loads:
        load.start()
    for k in range(1, PEERS):
        pl.semaphore_signal(barrier, inc=1, device_id=(ctx_peer(k), head), device_id_type=MESH)
    for k in range(1, SIDE):
        pl.semaphore_signal(barrier, inc=1, device_id=(ctx, y_peer(k)), device_id_type=MESH)
        pl.semaphore_signal(barrier, inc=1, device_id=(ctx, x_peer(k)), device_id_type=MESH)

    def remote(src, dst, send, recv, target):
        return pltpu.make_async_remote_copy(
            src_ref=src, dst_ref=dst, send_sem=send, recv_sem=recv, device_id=target, device_id_type=MESH
        )

    def finish_sends(ref, sem):
        remote(ref, ref, sem, sem, (ctx, head)).wait_send()

    def finish_arrivals(ref, sem):
        remote(ref, ref, sem, sem, (ctx, head)).wait_recv()

    root_head, root_chip = lax.div(chip, CHIPS // 2), lax.rem(chip, CHIPS // 2)
    is_root = root_chip < 2
    column = 2 * root_chip + core

    def o_copy(h, r):
        return remote(o_ref.at[h, r], o_all.at[ctx], o_send, o_recv, (PEERS // 2 * h + r, head))

    def root_of(h):
        return (ctx >= PEERS // 2 * h) & (ctx < PEERS // 2 * h + ROOTS)

    def m_slot(source, g):
        return m_all.at[pl.ds(LOCAL * source + GROUP * g, GROUP)]

    def at(h, p, c):
        return 2 * lax.rem(CHIPS // 2 * h + p, CHIPS) + c

    def m_leave(h, g):
        p = lax.rem(chip + CHIPS - CHIPS // 2 * h, CHIPS)
        mine = m_ref.at[h, pl.ds(GROUP * g, GROUP)]

        @pl.when(p < 2)
        def _():
            remote(mine, m_slot(ctx, g), m_send, m_recv.at[2 * p + g], (at(h, 1 - p, core), head)).start()
            remote(mine, m_slot(ctx, g), m_send, m_pass, (sibling, head)).start()

        @pl.when(p >= 2)
        def _():
            to = at(h, lax.div(CHIPS - 1 - p, 3), core)
            remote(mine, m_slot(ctx, g), m_send, m_recv.at[2 * p + g], (to, head)).start()

    def m_share(side, d, g, onward):
        p = lax.rem(side + (2 * side - 1) * d + CHIPS, CHIPS)
        slot = m_slot(at(root_head, p, core), g)
        copy = remote(slot, slot, m_send, m_recv.at[2 * p + g], (at(root_head, 1 - root_chip, core), head))
        copy.wait_recv()
        if onward:
            copy.start()
        remote(slot, slot, m_send, m_pass, (sibling, head)).start()

    def near(d, g):
        m_share(root_chip, d, g, True)

    def far(d, g):
        m_share(1 - root_chip, d, g, False)

    def attend_locally(chains):
        for c in chains:
            i, h = c["i"], c["h"]
            local = product(split(c["attend"]), split(c["solved"]))
            lo_ref[h, i] = local[:, :DV]
            ql_ref[h, i] = c["grown"] - local[:, DV:]

    def w_half(half):
        return w_ref.at[:, pl.ds(pl.multiple_of(half * (MODEL // 2), MODEL // 2), MODEL // 2)]

    def pick(over_x, over_y):
        return core * over_x + (1 - core) * over_y

    def w_copy(k):
        to = pick(x_peer(k), y_peer(k))
        return remote(w_half(core), w_all.at[core, pick(side_x, side_y)], w_send, w_recv, (ctx, to))

    def w_pass(k):
        slot = w_all.at[core, lax.rem(pick(side_x, side_y) + k, SIDE)]
        return remote(slot, slot, c_send, c_recv, (sibling, head))

    row = lax.broadcasted_iota(jnp.int32, (SPAN, SPAN), 0)
    col = lax.broadcasted_iota(jnp.int32, (SPAN, SPAN), 1)
    differ = row ^ col
    incl = row >= col
    strict = row > col
    tri = incl.astype(F32).astype(BF16)
    masks = [((differ >= s) & (differ < 2 * s)).astype(F32).astype(BF16) for s in (2, 4, 8, 16, 32, 64)]
    first = (differ == 1).astype(F32)
    eye = (row == col).astype(F32)
    d_ref[...] = jnp.zeros((HEADS, SLICE, DK), F32)
    everything = []

    for load in loads[:5]:
        load.wait()
    for g in range(LOCAL // GROUP):
        chains = []
        for i in range(g * GROUP, (g + 1) * GROUP):
            rows = pl.ds(i * SPAN, SPAN)
            q = q_ref[rows, :]
            k = k_ref[rows, :]
            qf = q.astype(F32)
            kf = k.astype(F32)
            rq = lax.rsqrt(jnp.sum(qf * qf, axis=-1, keepdims=True) + 1e-6) * DK**-0.5
            rk = lax.rsqrt(jnp.sum(kf * kf, axis=-1, keepdims=True) + 1e-6)
            rk_wide = spread_lanes(rk)
            rk_row = rk_wide.T
            both = mm_t(jnp.concatenate([k, q], axis=0), k)
            kk = both[:SPAN] * rk_wide * rk_row
            qk = both[SPAN:] * spread_lanes(rq) * rk_row
            kt = k.T
            shared = (qf * rq, kf, jnp.concatenate([kt, kt], axis=1), rk_wide, kk, qk)
            logits = beta_ref[:, rows].astype(F32)
            decays = decay_ref[:, rows].astype(F32)
            for h in range(HEADS):
                chains.append(
                    block_terms(
                        i, h, q, k, logits[h : h + 1], decays[h : h + 1],
                        v_ref[rows, h * DV : (h + 1) * DV].astype(F32), shared, (tri, strict, incl),
                    )
                )
        for c in chains:
            c["parts"] = split(c["lower"])
            c["inverse"] = eye - c["lower"] * first
        for mask in masks:
            for c in chains:
                c["halves"] = split(c["inverse"])
                off = (c["parts"][0] * mask, c["parts"][1] * mask)
                c["inner"] = product(off, c["halves"])
            for c in chains:
                c["inverse"] = c["inverse"] - product(c["halves"], split(c["inner"]))
        for c in chains:
            c["solved"] = product(split(c["inverse"]), split(c["rhs"]))
        for c in chains:
            tail2 = jnp.concatenate([c["tail"], c["tail"]], axis=1)
            high, low = split(tail2 * c["solved"])
            shift = mm(c["kt2"], jnp.concatenate([high, low], axis=0))
            i, h = c["i"], c["h"]
            m_ref[h, i] = shift[:, DV:].T.astype(BF16)
            o_ref[h, :, i] = shift[:, :DV].T.reshape(ROOTS, SLICE, DK).astype(BF16)
            decay = c["decay"].astype(BF16).astype(F32)
            d_ref[h, i : i + 1, :] = decay
            d_ref[h, 8 + i : 9 + i, :] = c["decay"] - decay
        everything += chains
        if g == 0:
            pl.semaphore_wait(barrier, PEERS - 1 + 2 * (SIDE - 1))
        for h in range(HEADS):
            m_leave(h, g)
        if g == 0:
            for k in range(1, SIDE):
                w_copy(k).start()
            w_own = [
                pltpu.make_async_copy(w_half(half), w_all.at[half, side], w_local.at[half])
                for half, side in enumerate((side_y, side_x))
            ]
            for copy in w_own:
                copy.start()

    @pl.when(is_root)
    def _():
        near(1, 0)
        far(0, 0)
        near(2, 0)

    for h in range(HEADS):
        o_ref[h, :, LOCAL] = jnp.broadcast_to(d_ref[h].astype(BF16), (ROOTS, SLICE, DK))
        for r in range(ROOTS):

            @pl.when(ctx != PEERS // 2 * h + r)
            def _():
                o_copy(h, r).start()

    attend_locally(everything[: len(everything) // 2])

    @pl.when(is_root)
    def _():
        m_all[pl.ds(LOCAL * ctx, LOCAL)] = m_ref[root_head]
        o_all[ctx] = o_ref[root_head, column]
        far(1, 0)
        near(3, 0)
        far(2, 0)
        near(1, 1)
        far(3, 0)

    attend_locally(everything[len(everything) // 2 :])

    lanes = lax.broadcasted_iota(jnp.int32, (1, SPAN), 1)
    found = jnp.zeros((1, SPAN), jnp.int32)
    for t in range(BLOCKS):
        found = jnp.where(lanes == arr_ref[t], t, found)
    inv_vmem[...] = found
    inv_copy = pltpu.make_async_copy(inv_vmem, inv_ref, inv_sem)
    inv_copy.start()
    bits = jnp.int32(0)
    start = prompt_ref[0]
    for i in range(1, 7):
        bits = bits | (jnp.int32(1) << start)
        start = start + prompt_ref[i]

    def chains_here():
        far(0, 1)
        near(2, 1)
        far(1, 1)
        near(3, 1)
        far(2, 1)
        far(3, 1)
        finish_arrivals(m_all.at[pl.ds(0, LOCAL * CHIPS)], m_pass)
        finish_arrivals(o_all.at[pl.ds(0, PEERS - 1)], o_recv)
        for source in range(PEERS):
            tile = o_all[source, LOCAL, :16].astype(F32)
            d_all[source * 8 : source * 8 + 8, :] = tile[:8] + tile[8:]
        def advance(state, t):
            slot = arr_ref[t]
            stream[t] = state.astype(BF16)
            high, low = split(state)
            moved = mm(jnp.concatenate([high, low], axis=0), m_all[slot])
            source, i = lax.div(slot, LOCAL), lax.rem(slot, LOCAL)
            decay = d_all[pl.ds(source * 8 + i, 1), :]
            return decay * state + o_all[source, i].astype(F32) - (moved[:SLICE] + moved[SLICE:])

        def step(t, pair):
            keep = (1 - ((bits >> t) & 1)).astype(F32)
            return advance(keep * pair[0], t), advance(pair[1], t + CHAIN)

        empty = jnp.zeros((SLICE, DK), F32)
        lax.fori_loop(0, CHAIN, step, (empty, empty), unroll=16)

        def place(a, carry):
            states[a] = stream[inv_ref[0, a]]
            return carry

        lax.fori_loop(0, BLOCKS, place, 0, unroll=8)

        mine = entry.at[root_head, :, pl.ds(pl.multiple_of(SLICE * column, SLICE), SLICE), :]
        for k in range(1, PEERS):
            to = ctx_peer(k)
            remote(
                states.at[pl.ds(LOCAL * to, LOCAL)], mine, s_send, s_recv.at[root_head], (to, head)
            ).start()
        mine[...] = states[pl.ds(LOCAL * ctx, LOCAL)]

    inv_copy.wait()
    pl.when(is_root)(chains_here)
    for copy in w_own:
        copy.wait()
    finish_arrivals(w_all.at[0, pl.ds(0, SIDE - 1)], w_recv)
    for k in range(1, SIDE):
        w_pass(k).start()
    for load in loads[5:]:
        load.wait()
    for h in range(HEADS):

        @pl.when(root_of(h))
        def _():
            finish_arrivals(states.at[pl.ds(0, LOCAL * (ROOTS - 1))], s_recv.at[h])

        @pl.when(jnp.logical_not(root_of(h)))
        def _():
            finish_arrivals(states.at[pl.ds(0, LOCAL * ROOTS)], s_recv.at[h])

    def n_copy(k):
        return remote(
            normed.at[:, lax.rem(side_y + k, SIDE)], rows_all.at[0, side_y], n_send, n_recv, (ctx, y_peer(k))
        )

    def r_copy(i):
        return remote(normed.at[i], rows_all.at[1, side_x], r_send, r_recv, (ctx, i * SIDE + side_y))

    gain = gain_ref[...]
    for i in range(LOCAL):
        for h in range(HEADS):
            high, low = split(ql_ref[h, i])
            state = entry[h, i]
            both = mm_t(jnp.concatenate([high, low], axis=0), state)
            core_out = both[:SPAN] + both[SPAN:] + lo_ref[h, i]
            scale = lax.rsqrt(jnp.mean(core_out * core_out, axis=-1, keepdims=True) + 1e-6)
            gate = gate_ref[i * SPAN : (i + 1) * SPAN, h * DV : (h + 1) * DV].astype(F32)
            value = core_out * scale * gain * (gate / (1.0 + jnp.exp(-gate)))
            normed[i, :, :, h * DV : (h + 1) * DV] = value.astype(BF16).reshape(SIDE, 32, DV)

        @pl.when(i != side_x)
        def _():
            r_copy(i).start()

    for k in range(1, SIDE):
        n_copy(k).start()
    rows_all[0, side_y] = normed[:, side_y]
    rows_all[1, side_x] = normed[side_x]
    finish_arrivals(w_all.at[0, pl.ds(0, SIDE - 1)], c_recv)
    finish_arrivals(rows_all.at[0, pl.ds(0, SIDE - 1)], n_recv)

    def p_copy(piece, k):
        if piece < PIECES // 2:
            source, to = lax.rem(side_x + k, SIDE), x_peer(k)
        else:
            source, to = lax.rem(side_y + k, SIDE), y_peer(k)
        return remote(
            part.at[piece, source], got.at[piece, k],
            p_send, p_recv.at[piece], (ctx, to),
        )

    for piece in range(PIECES):
        half, off = divmod(piece * PIECE, MODEL // 2)
        if piece == PIECES // 2:
            finish_arrivals(rows_all.at[1, pl.ds(0, SIDE - 1)], r_recv)
        if off == 0:
            left = jnp.concatenate(
                [rows_all[half, n].reshape(SPAN, HEADS * DV) for n in range(SIDE)], axis=1
            )
        right = w_all[half, :, :, off : off + PIECE].reshape(SIDE * HEADS * DV, PIECE)
        total = mm(left, right)
        part[piece] = total.astype(BF16).reshape(SIDE, 32, PIECE)
        for k in range(1, SIDE):
            p_copy(piece, k).start()
    for piece in range(PIECES):
        total = part[piece, side_x if piece < PIECES // 2 else side_y].astype(F32)
        finish_arrivals(got.at[piece, pl.ds(1, SIDE - 1)], p_recv.at[piece])
        for k in range(1, SIDE):
            total = total + got[piece, k].astype(F32)
        out_ref[:, piece * PIECE : (piece + 1) * PIECE] = total.astype(BF16)
    @pl.when(is_root)
    def _():
        finish_sends(m_all.at[pl.ds(0, 26 * GROUP)], m_send)
        finish_sends(o_all.at[pl.ds(0, HEADS * ROOTS - 1)], o_send)
        finish_sends(states.at[pl.ds(0, LOCAL * (PEERS - 1))], s_send)

    @pl.when(jnp.logical_not(is_root))
    def _():
        finish_sends(m_all.at[pl.ds(0, 4 * GROUP)], m_send)
        finish_sends(o_all.at[pl.ds(0, HEADS * ROOTS)], o_send)

    finish_sends(w_all.at[0, pl.ds(0, SIDE - 1)], w_send)
    finish_sends(w_all.at[0, pl.ds(0, SIDE - 1)], c_send)
    finish_sends(rows_all.at[0, pl.ds(0, SIDE - 1)], n_send)
    finish_sends(rows_all.at[1, pl.ds(0, SIDE - 1)], r_send)
    finish_sends(part.at[pl.ds(0, PIECES - 1)], p_send)


def per_device(q_rows, k_rows, v_rows, gate_rows, beta_logits, log_decay, norm_gain, out_weight, prompt_blocks, arrival_slot):
    smem = pl.BlockSpec(memory_space=pltpu.SMEM)
    vmem = pl.BlockSpec(memory_space=pltpu.VMEM)
    whole = pl.BlockSpec(memory_space=pl.ANY)
    tokens = LOCAL * SPAN
    dma = pltpu.SemaphoreType.DMA
    return pl.pallas_call(
        main_kernel,
        out_shape=pltpu.VMEM((tokens // PEERS, MODEL), BF16),
        in_specs=[smem, smem] + [whole] * 8,
        out_specs=vmem,
        scratch_shapes=[
            pltpu.VMEM((tokens, DK), BF16),
            pltpu.VMEM((tokens, DK), BF16),
            pltpu.VMEM((tokens, HEADS * DV), BF16),
            pltpu.VMEM((tokens, HEADS * DV), BF16),
            pltpu.VMEM((HEADS, tokens), BF16),
            pltpu.VMEM((HEADS, tokens), BF16),
            pltpu.VMEM((1, DV), F32),
            pltpu.VMEM((HEADS, LOCAL, DK, DK), BF16),
            pltpu.VMEM((HEADS, ROOTS, LOCAL + 1, SLICE, DK), BF16),
            pltpu.VMEM((HEADS, SLICE, DK), F32),
            pltpu.VMEM((HEADS, LOCAL, SPAN, DK), F32),
            pltpu.VMEM((HEADS, LOCAL, SPAN, DV), F32),
            pltpu.VMEM((1, SPAN), jnp.int32),
            pltpu.SMEM((1, SPAN), jnp.int32),
            pltpu.VMEM((BLOCKS, DK, DK), BF16),
            pltpu.VMEM((PEERS, LOCAL + 1, SLICE, DK), BF16),
            pltpu.VMEM((PEERS * 8, DK), F32),
            pltpu.VMEM((BLOCKS, SLICE, DK), BF16),
            pltpu.VMEM((BLOCKS, SLICE, DK), BF16),
            pltpu.VMEM((HEADS, LOCAL, DV, DK), BF16),
            pltpu.VMEM((LOCAL, SIDE, 32, HEADS * DV), BF16),
            pltpu.VMEM((2, SIDE, LOCAL, 32, HEADS * DV), BF16),
            pltpu.VMEM((2, SIDE, HEADS * DV, MODEL // 2), BF16),
            pltpu.VMEM((PIECES, SIDE, 32, PIECE), BF16),
            pltpu.VMEM((PIECES, SIDE, 32, PIECE), BF16),
            dma((7,)), dma, dma, dma, dma((2,)), dma, dma,
            dma, dma((2 * CHIPS,)), dma, dma, dma,
            dma, dma((HEADS,)), dma, dma, dma, dma, dma, dma((PIECES,)),
        ],
        compiler_params=pltpu.CompilerParams(
            collective_id=0, has_side_effects=True, vmem_limit_bytes=VMEM_LIMIT
        ),
    )(
        arrival_slot, prompt_blocks, q_rows, k_rows, v_rows, gate_rows, beta_logits.T, log_decay.T,
        norm_gain.reshape(1, DV), out_weight,
    )


def solution(mesh):
    in_specs = (
        P("ctx", "head"),
        P("ctx", "head"),
        P("ctx", "head"),
        P("ctx", "head"),
        P("ctx", "head"),
        P("ctx", "head"),
        P(),
        P("head", None),
        P(),
        P(),
    )
    return jax.shard_map(
        per_device, mesh=mesh, in_specs=in_specs, out_specs=P(("ctx", "head"), None), check_vma=False
    )
```

```python
import jax
import jax.numpy as jnp
from jax import lax
from jax.experimental import pallas as pl
from jax.experimental.pallas import tpu as pltpu
from jax.sharding import PartitionSpec as P

SPAN = 128
DK = 128
DV = 128
HEADS = 2
LOCAL = 4
PEERS = 16
CHIPS = 8
SLICE = 16
BLOCKS = 64
CHAIN = 32
SIDE = 4
MODEL = 2048
PIECES = 4
PIECE = MODEL // PIECES
GROUP = 2
VMEM_LIMIT = 60 * 2**20
MESH = pl.DeviceIdType.MESH
F32 = jnp.float32
BF16 = jnp.bfloat16


def split(x):
    high = x.astype(BF16)
    return high, (x - high.astype(F32)).astype(BF16)


def mm(a, b):
    return jnp.dot(a, b, preferred_element_type=F32)


def mm_t(a, b):
    return lax.dot_general(a, b, (((1,), (1,)), ((), ())), preferred_element_type=F32)


def product(a, b):
    a_high, a_low = a
    b_high, b_low = b
    n = b_high.shape[1]
    if n == 128:
        left = jnp.concatenate([a_high, a_low], axis=1)
        right = jnp.concatenate(
            [
                jnp.concatenate([b_high, b_low], axis=1),
                jnp.concatenate([b_high, jnp.zeros_like(b_low)], axis=1),
            ],
            axis=0,
        )
        both = mm(left, right)
        return both[:, :n] + both[:, n:]
    left = jnp.concatenate([a_high, a_low], axis=1)
    right = jnp.concatenate([b_high, b_high], axis=0)
    return mm(left, right) + mm(a_high, b_low)


def spread_lanes(column):
    return jnp.broadcast_to(column, (column.shape[0], 128))


def block_terms(i, h, q, k, beta_row, decay_row, v, shared, consts):
    tri, strict, incl = consts
    qn, kf, kt2, rk_wide, kk, qk = shared
    beta = jnp.broadcast_to(1.0 / (1.0 + jnp.exp(-beta_row)), (SPAN, SPAN)).T
    steps = jnp.broadcast_to(decay_row, (SPAN, SPAN)).astype(BF16)
    wide = mm_t(tri, steps)
    wide_row = mm_t(steps, tri)
    ratio = jnp.exp(jnp.minimum(wide - wide_row, 0.0))
    lower = jnp.where(strict, beta * ratio * kk, 0.0)
    attend = jnp.where(incl, ratio * qk, 0.0)
    growth = jnp.exp(wide)
    end = wide[SPAN - 1 : SPAN, :]
    tail = jnp.exp(end - wide) * rk_wide
    rhs = jnp.concatenate([beta * v, beta * growth * rk_wide * kf], axis=1)
    return dict(i=i, h=h, lower=lower, attend=attend, tail=tail, rhs=rhs, kt2=kt2, grown=growth * qn, decay=jnp.exp(end))


def main_kernel(
    arr_ref, prompt_ref, q_hbm, k_hbm, v_hbm, gate_hbm, beta_hbm, decay_hbm, gain_hbm, w_ref,
    out_ref,
    q_ref, k_ref, v_ref, gate_ref, beta_ref, decay_ref, gain_ref,
    m_ref, o_ref, d_ref, ql_ref, lo_ref, inv_vmem, inv_ref,
    m_all, o_all, d_all, stream, states, entry, gated, normed, rows_all, w_all, part, got,
    in_sem, inv_sem, w_send, w_recv, w_local, c_send, c_recv, m_send, m_recv, o_send, o_recv,
    s_send, s_recv, n_send, n_recv, r_send, r_recv, p_send, p_recv,
):
    ctx = lax.axis_index("ctx")
    head = lax.axis_index("head")
    chip, core = lax.div(ctx, 2), lax.rem(ctx, 2)
    sibling = 2 * chip + 1 - core
    side_x, side_y = lax.div(head, SIDE), lax.rem(head, SIDE)

    def ctx_peer(k):
        return lax.rem(ctx + k, PEERS)

    def y_peer(k):
        return side_x * SIDE + lax.rem(side_y + k, SIDE)

    def x_peer(k):
        return lax.rem(side_x + k, SIDE) * SIDE + side_y

    barrier = pltpu.get_barrier_semaphore()

    loads = [
        pltpu.make_async_copy(src, dst, in_sem.at[n])
        for n, (src, dst) in enumerate(
            (
                (k_hbm, k_ref), (q_hbm, q_ref), (beta_hbm, beta_ref), (decay_hbm, decay_ref),
                (v_hbm, v_ref), (gate_hbm, gate_ref), (gain_hbm, gain_ref),
            )
        )
    ]
    for load in loads:
        load.start()
    for k in range(1, PEERS):
        pl.semaphore_signal(barrier, inc=1, device_id=(ctx_peer(k), head), device_id_type=MESH)
    for k in range(1, SIDE):
        pl.semaphore_signal(barrier, inc=1, device_id=(ctx, y_peer(k)), device_id_type=MESH)
        pl.semaphore_signal(barrier, inc=1, device_id=(ctx, x_peer(k)), device_id_type=MESH)

    def remote(src, dst, send, recv, target):
        return pltpu.make_async_remote_copy(
            src_ref=src, dst_ref=dst, send_sem=send, recv_sem=recv, device_id=target, device_id_type=MESH
        )

    def finish_sends(ref, sem):
        remote(ref, ref, sem, sem, (ctx, head)).wait_send()

    def finish_arrivals(ref, sem):
        remote(ref, ref, sem, sem, (ctx, head)).wait_recv()

    def o_copy(k):
        to = ctx_peer(k)
        return remote(o_ref.at[lax.rem(to, 2), lax.div(to, 2)], o_all.at[ctx], o_send, o_recv, (to, head))

    def m_slot(source, g):
        return m_all.at[pl.ds(LOCAL * source + GROUP * g, GROUP)]

    def m_near(z):
        return lax.rem(chip + z + CHIPS, CHIPS)

    def m_first(h, step, g):
        return remote(
            m_ref.at[h, pl.ds(GROUP * g, GROUP)], m_slot(ctx, g), m_send, m_recv.at[2 * ctx + g],
            (2 * m_near(step) + h, head),
        )

    def m_sibling(g):
        return remote(
            m_ref.at[1 - core, pl.ds(GROUP * g, GROUP)], m_slot(ctx, g), m_send, m_recv.at[2 * ctx + g],
            (sibling, head),
        )

    def m_next(source, g, step):
        return remote(
            m_slot(source, g), m_slot(source, g), m_send, m_recv.at[2 * source + g],
            (2 * m_near(step) + core, head),
        )

    def forward(k, g):
        for step in (1, -1):
            for s in range(2):
                last = 4 if (s == 0) == (step == 1) else 3
                if k > last:
                    continue
                source = 2 * m_near(-step * k) + s
                m_next(source, g, step).wait_recv()
                if k < last:
                    m_next(source, g, step).start()

    def attend_locally(chains):
        for c in chains:
            i, h = c["i"], c["h"]
            local = product(split(c["attend"]), split(c["solved"]))
            lo_ref[h, i] = local[:, :DV]
            ql_ref[h, i] = c["grown"] - local[:, DV:]

    def w_half(half):
        return w_ref.at[:, pl.ds(pl.multiple_of(half * (MODEL // 2), MODEL // 2), MODEL // 2)]

    def pick(over_x, over_y):
        return core * over_x + (1 - core) * over_y

    def w_copy(k):
        to = pick(x_peer(k), y_peer(k))
        return remote(w_half(core), w_all.at[core, pick(side_x, side_y)], w_send, w_recv, (ctx, to))

    def w_pass(k):
        slot = w_all.at[core, lax.rem(pick(side_x, side_y) + k, SIDE)]
        return remote(slot, slot, c_send, c_recv, (sibling, head))

    row = lax.broadcasted_iota(jnp.int32, (SPAN, SPAN), 0)
    col = lax.broadcasted_iota(jnp.int32, (SPAN, SPAN), 1)
    differ = row ^ col
    incl = row >= col
    strict = row > col
    tri = incl.astype(F32).astype(BF16)
    masks = [((differ >= s) & (differ < 2 * s)).astype(F32).astype(BF16) for s in (2, 4, 8, 16, 32, 64)]
    first = (differ == 1).astype(F32)
    eye = (row == col).astype(F32)
    d_ref[...] = jnp.zeros((HEADS, SLICE, DK), F32)
    everything = []

    for load in loads[:5]:
        load.wait()
    for g in range(LOCAL // GROUP):
        chains = []
        for i in range(g * GROUP, (g + 1) * GROUP):
            rows = pl.ds(i * SPAN, SPAN)
            q = q_ref[rows, :]
            k = k_ref[rows, :]
            qf = q.astype(F32)
            kf = k.astype(F32)
            rq = lax.rsqrt(jnp.sum(qf * qf, axis=-1, keepdims=True) + 1e-6) * DK**-0.5
            rk = lax.rsqrt(jnp.sum(kf * kf, axis=-1, keepdims=True) + 1e-6)
            rk_wide = spread_lanes(rk)
            rk_row = rk_wide.T
            both = mm_t(jnp.concatenate([k, q], axis=0), k)
            kk = both[:SPAN] * rk_wide * rk_row
            qk = both[SPAN:] * spread_lanes(rq) * rk_row
            kt = k.T
            shared = (qf * rq, kf, jnp.concatenate([kt, kt], axis=1), rk_wide, kk, qk)
            logits = beta_ref[:, rows].astype(F32)
            decays = decay_ref[:, rows].astype(F32)
            for h in range(HEADS):
                chains.append(
                    block_terms(
                        i, h, q, k, logits[h : h + 1], decays[h : h + 1],
                        v_ref[rows, h * DV : (h + 1) * DV].astype(F32), shared, (tri, strict, incl),
                    )
                )
        for c in chains:
            c["parts"] = split(c["lower"])
            c["inverse"] = eye - c["lower"] * first
        for mask in masks:
            for c in chains:
                c["halves"] = split(c["inverse"])
                off = (c["parts"][0] * mask, c["parts"][1] * mask)
                c["inner"] = product(off, c["halves"])
            for c in chains:
                c["inverse"] = c["inverse"] - product(c["halves"], split(c["inner"]))
        for c in chains:
            c["solved"] = product(split(c["inverse"]), split(c["rhs"]))
        for c in chains:
            tail2 = jnp.concatenate([c["tail"], c["tail"]], axis=1)
            high, low = split(tail2 * c["solved"])
            shift = mm(c["kt2"], jnp.concatenate([high, low], axis=0))
            i, h = c["i"], c["h"]
            m_ref[h, i] = shift[:, DV:].T.astype(BF16)
            o_ref[h, :, i] = shift[:, :DV].T.reshape(CHIPS, SLICE, DK).astype(BF16)
            decay = c["decay"].astype(BF16).astype(F32)
            d_ref[h, i : i + 1, :] = decay
            d_ref[h, 8 + i : 9 + i, :] = c["decay"] - decay
        everything += chains
        if g == 0:
            pl.semaphore_wait(barrier, PEERS - 1 + 2 * (SIDE - 1))
        for h, step in ((0, 1), (0, -1), (1, 1), (1, -1)):
            m_first(h, step, g).start()
        m_sibling(g).start()

    forward(1, 0)
    for h in range(HEADS):
        o_ref[h, :, LOCAL] = jnp.broadcast_to(d_ref[h].astype(BF16), (CHIPS, SLICE, DK))
    for k in range(1, PEERS):
        o_copy(k).start()
    m_all[pl.ds(LOCAL * ctx, LOCAL)] = m_ref[core]
    o_all[ctx] = o_ref[core, chip]
    forward(1, 1)
    attend_locally(everything[: len(everything) // 2])
    forward(2, 0)
    attend_locally(everything[len(everything) // 2 :])
    forward(2, 1)

    lanes = lax.broadcasted_iota(jnp.int32, (1, SPAN), 1)
    found = jnp.zeros((1, SPAN), jnp.int32)
    for t in range(BLOCKS):
        found = jnp.where(lanes == arr_ref[t], t, found)
    inv_vmem[...] = found
    inv_copy = pltpu.make_async_copy(inv_vmem, inv_ref, inv_sem)
    inv_copy.start()
    bits = jnp.int32(0)
    start = prompt_ref[0]
    for i in range(1, 7):
        bits = bits | (jnp.int32(1) << start)
        start = start + prompt_ref[i]

    forward(3, 0)
    forward(3, 1)
    for k in range(1, SIDE):
        w_copy(k).start()
    w_own = [
        pltpu.make_async_copy(w_half(half), w_all.at[half, side], w_local.at[half])
        for half, side in enumerate((side_y, side_x))
    ]
    for copy in w_own:
        copy.start()
    forward(4, 0)
    forward(4, 1)
    for g in range(LOCAL // GROUP):
        m_next(sibling, g, 0).wait_recv()
    finish_arrivals(o_all.at[pl.ds(0, PEERS - 1)], o_recv)
    for source in range(PEERS):
        tile = o_all[source, LOCAL].astype(F32)
        d_all[source * 8 : source * 8 + 8, :] = tile[:8] + tile[8:]
    inv_copy.wait()

    def advance(state, t):
        slot = arr_ref[t]
        stream[t] = state.astype(BF16)
        high, low = split(state)
        moved = mm(jnp.concatenate([high, low], axis=0), m_all[slot])
        source, i = lax.div(slot, LOCAL), lax.rem(slot, LOCAL)
        decay = d_all[pl.ds(source * 8 + i, 1), :]
        return decay * state + o_all[source, i].astype(F32) - (moved[:SLICE] + moved[SLICE:])

    def step(t, pair):
        keep = (1 - ((bits >> t) & 1)).astype(F32)
        return advance(keep * pair[0], t), advance(pair[1], t + CHAIN)

    empty = jnp.zeros((SLICE, DK), F32)
    lax.fori_loop(0, CHAIN, step, (empty, empty), unroll=16)

    def place(a, carry):
        states[a] = stream[inv_ref[0, a]]
        return carry

    lax.fori_loop(0, BLOCKS, place, 0, unroll=8)

    def s_rows(h, z):
        return entry.at[h, :, pl.ds(pl.multiple_of(SLICE * z, SLICE), SLICE), :]

    def s_copy(k):
        to = ctx_peer(k)
        return remote(states.at[pl.ds(LOCAL * to, LOCAL)], s_rows(core, chip), s_send, s_recv, (to, head))

    for k in range(1, PEERS):
        s_copy(k).start()
    entry[core, :, pl.ds(pl.multiple_of(SLICE * chip, SLICE), SLICE), :] = states[pl.ds(LOCAL * ctx, LOCAL)]
    for load in loads[5:]:
        load.wait()
    gain = jnp.concatenate([gain_ref[...]] * HEADS, axis=1)
    for i in range(LOCAL):
        gate = gate_ref[i * SPAN : (i + 1) * SPAN, :].astype(F32)
        gated[i] = gain * (gate / (1.0 + jnp.exp(-gate)))
    for copy in w_own:
        copy.wait()
    finish_arrivals(w_all.at[0, pl.ds(0, SIDE - 1)], w_recv)
    for k in range(1, SIDE):
        w_pass(k).start()
    finish_arrivals(states.at[pl.ds(0, LOCAL * (PEERS - 1))], s_recv)

    def n_copy(k):
        return remote(
            normed.at[:, lax.rem(side_y + k, SIDE)], rows_all.at[0, side_y], n_send, n_recv, (ctx, y_peer(k))
        )

    def r_copy(i):
        return remote(normed.at[i], rows_all.at[1, side_x], r_send, r_recv, (ctx, i * SIDE + side_y))

    for i in range(LOCAL):
        for h in range(HEADS):
            high, low = split(ql_ref[h, i])
            state = entry[h, i]
            both = mm_t(jnp.concatenate([high, low], axis=0), state)
            core_out = both[:SPAN] + both[SPAN:] + lo_ref[h, i]
            scale = lax.rsqrt(jnp.mean(core_out * core_out, axis=-1, keepdims=True) + 1e-6)
            value = core_out * scale * gated[i, :, h * DV : (h + 1) * DV]
            normed[i, :, :, h * DV : (h + 1) * DV] = value.astype(BF16).reshape(SIDE, 32, DV)

        @pl.when(i != side_x)
        def _():
            r_copy(i).start()

    for k in range(1, SIDE):
        n_copy(k).start()
    rows_all[0, side_y] = normed[:, side_y]
    rows_all[1, side_x] = normed[side_x]
    finish_arrivals(w_all.at[0, pl.ds(0, SIDE - 1)], c_recv)
    finish_arrivals(rows_all.at[0, pl.ds(0, SIDE - 1)], n_recv)

    def p_copy(piece, k):
        if piece < PIECES // 2:
            source, to = lax.rem(side_x + k, SIDE), x_peer(k)
        else:
            source, to = lax.rem(side_y + k, SIDE), y_peer(k)
        return remote(
            part.at[piece, source], got.at[piece, k],
            p_send, p_recv.at[piece], (ctx, to),
        )

    for piece in range(PIECES):
        half, off = divmod(piece * PIECE, MODEL // 2)
        if piece == PIECES // 2:
            finish_arrivals(rows_all.at[1, pl.ds(0, SIDE - 1)], r_recv)
        if off == 0:
            left = jnp.concatenate(
                [rows_all[half, n].reshape(SPAN, HEADS * DV) for n in range(SIDE)], axis=1
            )
        right = w_all[half, :, :, off : off + PIECE].reshape(SIDE * HEADS * DV, PIECE)
        total = mm(left, right)
        part[piece] = total.astype(BF16).reshape(SIDE, 32, PIECE)
        for k in range(1, SIDE):
            p_copy(piece, k).start()
    for piece in range(PIECES):
        total = part[piece, side_x if piece < PIECES // 2 else side_y].astype(F32)
        finish_arrivals(got.at[piece, pl.ds(1, SIDE - 1)], p_recv.at[piece])
        for k in range(1, SIDE):
            total = total + got[piece, k].astype(F32)
        out_ref[:, piece * PIECE : (piece + 1) * PIECE] = total.astype(BF16)
    finish_sends(m_all.at[pl.ds(0, LOCAL * (PEERS - 1))], m_send)
    finish_sends(o_all.at[pl.ds(0, PEERS - 1)], o_send)
    finish_sends(states.at[pl.ds(0, LOCAL * (PEERS - 1))], s_send)
    finish_sends(w_all.at[0, pl.ds(0, SIDE - 1)], w_send)
    finish_sends(w_all.at[0, pl.ds(0, SIDE - 1)], c_send)
    finish_sends(rows_all.at[0, pl.ds(0, SIDE - 1)], n_send)
    finish_sends(rows_all.at[1, pl.ds(0, SIDE - 1)], r_send)
    finish_sends(part.at[pl.ds(0, PIECES - 1)], p_send)


def per_device(q_rows, k_rows, v_rows, gate_rows, beta_logits, log_decay, norm_gain, out_weight, prompt_blocks, arrival_slot):
    smem = pl.BlockSpec(memory_space=pltpu.SMEM)
    vmem = pl.BlockSpec(memory_space=pltpu.VMEM)
    whole = pl.BlockSpec(memory_space=pl.ANY)
    tokens = LOCAL * SPAN
    dma = pltpu.SemaphoreType.DMA
    return pl.pallas_call(
        main_kernel,
        out_shape=pltpu.VMEM((tokens // PEERS, MODEL), BF16),
        in_specs=[smem, smem] + [whole] * 8,
        out_specs=vmem,
        scratch_shapes=[
            pltpu.VMEM((tokens, DK), BF16),
            pltpu.VMEM((tokens, DK), BF16),
            pltpu.VMEM((tokens, HEADS * DV), BF16),
            pltpu.VMEM((tokens, HEADS * DV), BF16),
            pltpu.VMEM((HEADS, tokens), BF16),
            pltpu.VMEM((HEADS, tokens), BF16),
            pltpu.VMEM((1, DV), F32),
            pltpu.VMEM((HEADS, LOCAL, DK, DK), BF16),
            pltpu.VMEM((HEADS, CHIPS, LOCAL + 1, SLICE, DK), BF16),
            pltpu.VMEM((HEADS, SLICE, DK), F32),
            pltpu.VMEM((HEADS, LOCAL, SPAN, DK), F32),
            pltpu.VMEM((HEADS, LOCAL, SPAN, DV), F32),
            pltpu.VMEM((1, SPAN), jnp.int32),
            pltpu.SMEM((1, SPAN), jnp.int32),
            pltpu.VMEM((BLOCKS, DK, DK), BF16),
            pltpu.VMEM((PEERS, LOCAL + 1, SLICE, DK), BF16),
            pltpu.VMEM((PEERS * 8, DK), F32),
            pltpu.VMEM((BLOCKS, SLICE, DK), BF16),
            pltpu.VMEM((BLOCKS, SLICE, DK), BF16),
            pltpu.VMEM((HEADS, LOCAL, DV, DK), BF16),
            pltpu.VMEM((LOCAL, SPAN, HEADS * DV), F32),
            pltpu.VMEM((LOCAL, SIDE, 32, HEADS * DV), BF16),
            pltpu.VMEM((2, SIDE, LOCAL, 32, HEADS * DV), BF16),
            pltpu.VMEM((2, SIDE, HEADS * DV, MODEL // 2), BF16),
            pltpu.VMEM((PIECES, SIDE, 32, PIECE), BF16),
            pltpu.VMEM((PIECES, SIDE, 32, PIECE), BF16),
            dma((7,)), dma, dma, dma, dma((2,)), dma, dma,
            dma, dma((2 * PEERS,)), dma, dma,
            dma, dma, dma, dma, dma, dma, dma, dma((PIECES,)),
        ],
        compiler_params=pltpu.CompilerParams(
            collective_id=0, has_side_effects=True, vmem_limit_bytes=VMEM_LIMIT
        ),
    )(
        arrival_slot, prompt_blocks, q_rows, k_rows, v_rows, gate_rows, beta_logits.T, log_decay.T,
        norm_gain.reshape(1, DV), out_weight,
    )


def solution(mesh):
    in_specs = (
        P("ctx", "head"),
        P("ctx", "head"),
        P("ctx", "head"),
        P("ctx", "head"),
        P("ctx", "head"),
        P("ctx", "head"),
        P(),
        P("head", None),
        P(),
        P(),
    )
    return jax.shard_map(
        per_device, mesh=mesh, in_specs=in_specs, out_specs=P(("ctx", "head"), None), check_vma=False
    )
```

```python
import jax
import jax.numpy as jnp
from jax import lax
from jax.experimental import pallas as pl
from jax.experimental.pallas import tpu as pltpu
from jax.sharding import PartitionSpec as P

SPAN = 128
DK = 128
DV = 128
HEADS = 2
LOCAL = 4
PEERS = 16
CHIPS = 8
SLICE = 16
BLOCKS = 64
CHAIN = 32
SIDE = 4
MODEL = 2048
PIECES = 4
PIECE = MODEL // PIECES
GROUP = 2
VMEM_LIMIT = 60 * 2**20
MESH = pl.DeviceIdType.MESH
F32 = jnp.float32
BF16 = jnp.bfloat16


def split(x):
    high = x.astype(BF16)
    return high, (x - high.astype(F32)).astype(BF16)


def mm(a, b):
    return jnp.dot(a, b, preferred_element_type=F32)


def mm_t(a, b):
    return lax.dot_general(a, b, (((1,), (1,)), ((), ())), preferred_element_type=F32)


def product(a, b):
    a_high, a_low = a
    b_high, b_low = b
    n = b_high.shape[1]
    if n == 128:
        left = jnp.concatenate([a_high, a_low], axis=1)
        right = jnp.concatenate(
            [
                jnp.concatenate([b_high, b_low], axis=1),
                jnp.concatenate([b_high, jnp.zeros_like(b_low)], axis=1),
            ],
            axis=0,
        )
        both = mm(left, right)
        return both[:, :n] + both[:, n:]
    left = jnp.concatenate([a_high, a_low], axis=1)
    right = jnp.concatenate([b_high, b_high], axis=0)
    return mm(left, right) + mm(a_high, b_low)


def spread_lanes(column):
    return jnp.broadcast_to(column, (column.shape[0], 128))


def block_terms(i, h, q, k, beta_row, decay_row, v, shared, consts):
    tri, strict, incl = consts
    qn, kf, kt2, rk_wide, kk, qk = shared
    beta = jnp.broadcast_to(1.0 / (1.0 + jnp.exp(-beta_row)), (SPAN, SPAN)).T
    steps = jnp.broadcast_to(decay_row, (SPAN, SPAN)).astype(BF16)
    wide = mm_t(tri, steps)
    wide_row = mm_t(steps, tri)
    ratio = jnp.exp(jnp.minimum(wide - wide_row, 0.0))
    lower = jnp.where(strict, beta * ratio * kk, 0.0)
    attend = jnp.where(incl, ratio * qk, 0.0)
    growth = jnp.exp(wide)
    end = wide[SPAN - 1 : SPAN, :]
    tail = jnp.exp(end - wide) * rk_wide
    rhs = jnp.concatenate([beta * v, beta * growth * rk_wide * kf], axis=1)
    return dict(i=i, h=h, lower=lower, attend=attend, tail=tail, rhs=rhs, kt2=kt2, grown=growth * qn, decay=jnp.exp(end))


def main_kernel(
    arr_ref, prompt_ref, q_hbm, k_hbm, v_hbm, gate_hbm, beta_hbm, decay_hbm, gain_hbm, w_ref,
    out_ref,
    q_ref, k_ref, v_ref, gate_ref, beta_ref, decay_ref, gain_ref,
    m_ref, o_ref, d_ref, ql_ref, lo_ref, inv_vmem, inv_ref,
    m_all, o_all, d_all, stream, states, entry, gated, normed, rows_all, w_all, part, got,
    in_sem, inv_sem, w_send, w_recv, w_local, c_send, c_recv, m_send, m_recv, o_send, o_recv,
    s_send, s_recv, n_send, n_recv, r_send, r_recv, p_send, p_recv,
):
    ctx = lax.axis_index("ctx")
    head = lax.axis_index("head")
    chip, core = lax.div(ctx, 2), lax.rem(ctx, 2)
    sibling = 2 * chip + 1 - core
    side_x, side_y = lax.div(head, SIDE), lax.rem(head, SIDE)

    def ctx_peer(k):
        return lax.rem(ctx + k, PEERS)

    def y_peer(k):
        return side_x * SIDE + lax.rem(side_y + k, SIDE)

    def x_peer(k):
        return lax.rem(side_x + k, SIDE) * SIDE + side_y

    barrier = pltpu.get_barrier_semaphore()

    loads = [
        pltpu.make_async_copy(src, dst, in_sem.at[n])
        for n, (src, dst) in enumerate(
            (
                (k_hbm, k_ref), (q_hbm, q_ref), (beta_hbm, beta_ref), (decay_hbm, decay_ref),
                (v_hbm, v_ref), (gate_hbm, gate_ref), (gain_hbm, gain_ref),
            )
        )
    ]
    for load in loads:
        load.start()
    for k in range(1, PEERS):
        pl.semaphore_signal(barrier, inc=1, device_id=(ctx_peer(k), head), device_id_type=MESH)
    for k in range(1, SIDE):
        pl.semaphore_signal(barrier, inc=1, device_id=(ctx, y_peer(k)), device_id_type=MESH)
        pl.semaphore_signal(barrier, inc=1, device_id=(ctx, x_peer(k)), device_id_type=MESH)

    def remote(src, dst, send, recv, target):
        return pltpu.make_async_remote_copy(
            src_ref=src, dst_ref=dst, send_sem=send, recv_sem=recv, device_id=target, device_id_type=MESH
        )

    def finish_sends(ref, sem):
        remote(ref, ref, sem, sem, (ctx, head)).wait_send()

    def finish_arrivals(ref, sem):
        remote(ref, ref, sem, sem, (ctx, head)).wait_recv()

    def o_copy(k):
        to = ctx_peer(k)
        return remote(o_ref.at[lax.rem(to, 2), lax.div(to, 2)], o_all.at[ctx], o_send, o_recv, (to, head))

    def m_slot(source, g):
        return m_all.at[pl.ds(LOCAL * source + GROUP * g, GROUP)]

    def m_near(z):
        return lax.rem(chip + z + CHIPS, CHIPS)

    def m_first(h, step, g):
        return remote(
            m_ref.at[h, pl.ds(GROUP * g, GROUP)], m_slot(ctx, g), m_send, m_recv.at[2 * ctx + g],
            (2 * m_near(step) + h, head),
        )

    def m_sibling(g):
        return remote(
            m_ref.at[1 - core, pl.ds(GROUP * g, GROUP)], m_slot(ctx, g), m_send, m_recv.at[2 * ctx + g],
            (sibling, head),
        )

    def m_next(source, g, step):
        return remote(
            m_slot(source, g), m_slot(source, g), m_send, m_recv.at[2 * source + g],
            (2 * m_near(step) + core, head),
        )

    def forward(k, g):
        for step in (1, -1):
            for s in range(2):
                last = 4 if (s == 0) == (step == 1) else 3
                if k > last:
                    continue
                source = 2 * m_near(-step * k) + s
                m_next(source, g, step).wait_recv()
                if k < last:
                    m_next(source, g, step).start()

    def attend_locally(chains):
        for c in chains:
            i, h = c["i"], c["h"]
            local = product(split(c["attend"]), split(c["solved"]))
            lo_ref[h, i] = local[:, :DV]
            ql_ref[h, i] = c["grown"] - local[:, DV:]

    def w_half(half):
        return w_ref.at[:, pl.ds(pl.multiple_of(half * (MODEL // 2), MODEL // 2), MODEL // 2)]

    def pick(over_x, over_y):
        return core * over_x + (1 - core) * over_y

    def w_copy(k):
        to = pick(x_peer(k), y_peer(k))
        return remote(w_half(core), w_all.at[core, pick(side_x, side_y)], w_send, w_recv, (ctx, to))

    def w_pass(k):
        slot = w_all.at[core, lax.rem(pick(side_x, side_y) + k, SIDE)]
        return remote(slot, slot, c_send, c_recv, (sibling, head))

    row = lax.broadcasted_iota(jnp.int32, (SPAN, SPAN), 0)
    col = lax.broadcasted_iota(jnp.int32, (SPAN, SPAN), 1)
    differ = row ^ col
    incl = row >= col
    strict = row > col
    tri = incl.astype(F32).astype(BF16)
    masks = [((differ >= s) & (differ < 2 * s)).astype(F32).astype(BF16) for s in (2, 4, 8, 16, 32, 64)]
    first = (differ == 1).astype(F32)
    eye = (row == col).astype(F32)
    d_ref[...] = jnp.zeros((HEADS, SLICE, DK), F32)
    everything = []

    for load in loads[:5]:
        load.wait()
    for g in range(LOCAL // GROUP):
        chains = []
        for i in range(g * GROUP, (g + 1) * GROUP):
            rows = pl.ds(i * SPAN, SPAN)
            q = q_ref[rows, :]
            k = k_ref[rows, :]
            qf = q.astype(F32)
            kf = k.astype(F32)
            rq = lax.rsqrt(jnp.sum(qf * qf, axis=-1, keepdims=True) + 1e-6) * DK**-0.5
            rk = lax.rsqrt(jnp.sum(kf * kf, axis=-1, keepdims=True) + 1e-6)
            rk_wide = spread_lanes(rk)
            rk_row = rk_wide.T
            both = mm_t(jnp.concatenate([k, q], axis=0), k)
            kk = both[:SPAN] * rk_wide * rk_row
            qk = both[SPAN:] * spread_lanes(rq) * rk_row
            kt = k.T
            shared = (qf * rq, kf, jnp.concatenate([kt, kt], axis=1), rk_wide, kk, qk)
            logits = beta_ref[:, rows].astype(F32)
            decays = decay_ref[:, rows].astype(F32)
            for h in range(HEADS):
                chains.append(
                    block_terms(
                        i, h, q, k, logits[h : h + 1], decays[h : h + 1],
                        v_ref[rows, h * DV : (h + 1) * DV].astype(F32), shared, (tri, strict, incl),
                    )
                )
        for c in chains:
            c["parts"] = split(c["lower"])
            c["inverse"] = eye - c["lower"] * first
        for mask in masks:
            for c in chains:
                c["halves"] = split(c["inverse"])
                off = (c["parts"][0] * mask, c["parts"][1] * mask)
                c["inner"] = product(off, c["halves"])
            for c in chains:
                c["inverse"] = c["inverse"] - product(c["halves"], split(c["inner"]))
        for c in chains:
            c["solved"] = product(split(c["inverse"]), split(c["rhs"]))
        for c in chains:
            tail2 = jnp.concatenate([c["tail"], c["tail"]], axis=1)
            high, low = split(tail2 * c["solved"])
            shift = mm(c["kt2"], jnp.concatenate([high, low], axis=0))
            i, h = c["i"], c["h"]
            m_ref[h, i] = shift[:, DV:].T.astype(BF16)
            o_ref[h, :, i] = shift[:, :DV].T.reshape(CHIPS, SLICE, DK).astype(BF16)
            decay = c["decay"].astype(BF16).astype(F32)
            d_ref[h, i : i + 1, :] = decay
            d_ref[h, 8 + i : 9 + i, :] = c["decay"] - decay
        everything += chains
        if g == 0:
            pl.semaphore_wait(barrier, PEERS - 1 + 2 * (SIDE - 1))
        for h, step in ((0, 1), (0, -1), (1, 1), (1, -1)):
            m_first(h, step, g).start()
        m_sibling(g).start()

    forward(1, 0)
    for h in range(HEADS):
        o_ref[h, :, LOCAL] = jnp.broadcast_to(d_ref[h].astype(BF16), (CHIPS, SLICE, DK))
    for k in range(1, PEERS):
        o_copy(k).start()
    m_all[pl.ds(LOCAL * ctx, LOCAL)] = m_ref[core]
    o_all[ctx] = o_ref[core, chip]
    attend_locally(everything[: len(everything) // 2])
    forward(1, 1)
    forward(2, 0)
    attend_locally(everything[len(everything) // 2 :])
    forward(2, 1)

    lanes = lax.broadcasted_iota(jnp.int32, (1, SPAN), 1)
    found = jnp.zeros((1, SPAN), jnp.int32)
    for t in range(BLOCKS):
        found = jnp.where(lanes == arr_ref[t], t, found)
    inv_vmem[...] = found
    inv_copy = pltpu.make_async_copy(inv_vmem, inv_ref, inv_sem)
    inv_copy.start()
    bits = jnp.int32(0)
    start = prompt_ref[0]
    for i in range(1, 7):
        bits = bits | (jnp.int32(1) << start)
        start = start + prompt_ref[i]

    forward(3, 0)
    forward(3, 1)
    for k in range(1, SIDE):
        w_copy(k).start()
    w_own = [
        pltpu.make_async_copy(w_half(half), w_all.at[half, side], w_local.at[half])
        for half, side in enumerate((side_y, side_x))
    ]
    for copy in w_own:
        copy.start()
    forward(4, 0)
    forward(4, 1)
    for g in range(LOCAL // GROUP):
        m_next(sibling, g, 0).wait_recv()
    finish_arrivals(o_all.at[pl.ds(0, PEERS - 1)], o_recv)
    for source in range(PEERS):
        tile = o_all[source, LOCAL].astype(F32)
        d_all[source * 8 : source * 8 + 8, :] = tile[:8] + tile[8:]
    inv_copy.wait()

    def advance(state, t):
        slot = arr_ref[t]
        stream[t] = state.astype(BF16)
        high, low = split(state)
        moved = mm(jnp.concatenate([high, low], axis=0), m_all[slot])
        source, i = lax.div(slot, LOCAL), lax.rem(slot, LOCAL)
        decay = d_all[pl.ds(source * 8 + i, 1), :]
        return decay * state + o_all[source, i].astype(F32) - (moved[:SLICE] + moved[SLICE:])

    def step(t, pair):
        keep = (1 - ((bits >> t) & 1)).astype(F32)
        return advance(keep * pair[0], t), advance(pair[1], t + CHAIN)

    empty = jnp.zeros((SLICE, DK), F32)
    lax.fori_loop(0, CHAIN, step, (empty, empty), unroll=16)

    def place(to):
        for i in range(LOCAL):
            a = LOCAL * to + i
            states[a] = stream[inv_ref[0, a]]

    def s_rows(h, z):
        return entry.at[h, :, pl.ds(pl.multiple_of(SLICE * z, SLICE), SLICE), :]

    def s_copy(k):
        to = ctx_peer(k)
        return remote(states.at[pl.ds(LOCAL * to, LOCAL)], s_rows(core, chip), s_send, s_recv, (to, head))

    for k in range(1, PEERS):
        place(ctx_peer(k))
        s_copy(k).start()
    place(ctx)
    entry[core, :, pl.ds(pl.multiple_of(SLICE * chip, SLICE), SLICE), :] = states[pl.ds(LOCAL * ctx, LOCAL)]
    for load in loads[5:]:
        load.wait()
    gain = jnp.concatenate([gain_ref[...]] * HEADS, axis=1)
    for i in range(LOCAL):
        gate = gate_ref[i * SPAN : (i + 1) * SPAN, :].astype(F32)
        gated[i] = gain * (gate / (1.0 + jnp.exp(-gate)))
    for copy in w_own:
        copy.wait()
    finish_arrivals(w_all.at[0, pl.ds(0, SIDE - 1)], w_recv)
    for k in range(1, SIDE):
        w_pass(k).start()
    finish_arrivals(states.at[pl.ds(0, LOCAL * (PEERS - 1))], s_recv)

    def n_copy(k):
        return remote(
            normed.at[:, lax.rem(side_y + k, SIDE)], rows_all.at[0, side_y], n_send, n_recv, (ctx, y_peer(k))
        )

    def r_copy(i):
        return remote(normed.at[i], rows_all.at[1, side_x], r_send, r_recv, (ctx, i * SIDE + side_y))

    for i in range(LOCAL):
        for h in range(HEADS):
            high, low = split(ql_ref[h, i])
            state = entry[h, i]
            both = mm_t(jnp.concatenate([high, low], axis=0), state)
            core_out = both[:SPAN] + both[SPAN:] + lo_ref[h, i]
            scale = lax.rsqrt(jnp.mean(core_out * core_out, axis=-1, keepdims=True) + 1e-6)
            value = core_out * scale * gated[i, :, h * DV : (h + 1) * DV]
            normed[i, :, :, h * DV : (h + 1) * DV] = value.astype(BF16).reshape(SIDE, 32, DV)

        @pl.when(i != side_x)
        def _():
            r_copy(i).start()

    for k in range(1, SIDE):
        n_copy(k).start()
    rows_all[0, side_y] = normed[:, side_y]
    rows_all[1, side_x] = normed[side_x]
    finish_arrivals(w_all.at[0, pl.ds(0, SIDE - 1)], c_recv)

    def p_copy(piece, k):
        if piece < PIECES // 2:
            source, to = lax.rem(side_x + k, SIDE), x_peer(k)
        else:
            source, to = lax.rem(side_y + k, SIDE), y_peer(k)
        return remote(
            part.at[piece, source], got.at[piece, k],
            p_send, p_recv.at[piece], (ctx, to),
        )

    order = list(range(PIECES // 2, PIECES)) + list(range(PIECES // 2))
    for piece in order:
        half, off = divmod(piece * PIECE, MODEL // 2)
        if off == 0:
            finish_arrivals(rows_all.at[half, pl.ds(0, SIDE - 1)], r_recv if half else n_recv)
            left = jnp.concatenate(
                [rows_all[half, n].reshape(SPAN, HEADS * DV) for n in range(SIDE)], axis=1
            )
        right = w_all[half, :, :, off : off + PIECE].reshape(SIDE * HEADS * DV, PIECE)
        total = mm(left, right)
        part[piece] = total.astype(BF16).reshape(SIDE, 32, PIECE)
        for k in range(1, SIDE):
            p_copy(piece, k).start()
    for piece in order:
        total = part[piece, side_x if piece < PIECES // 2 else side_y].astype(F32)
        finish_arrivals(got.at[piece, pl.ds(1, SIDE - 1)], p_recv.at[piece])
        for k in range(1, SIDE):
            total = total + got[piece, k].astype(F32)
        out_ref[:, piece * PIECE : (piece + 1) * PIECE] = total.astype(BF16)
    finish_sends(m_all.at[pl.ds(0, LOCAL * (PEERS - 1))], m_send)
    finish_sends(o_all.at[pl.ds(0, PEERS - 1)], o_send)
    finish_sends(states.at[pl.ds(0, LOCAL * (PEERS - 1))], s_send)
    finish_sends(w_all.at[0, pl.ds(0, SIDE - 1)], w_send)
    finish_sends(w_all.at[0, pl.ds(0, SIDE - 1)], c_send)
    finish_sends(rows_all.at[0, pl.ds(0, SIDE - 1)], n_send)
    finish_sends(rows_all.at[1, pl.ds(0, SIDE - 1)], r_send)
    finish_sends(part.at[pl.ds(0, PIECES - 1)], p_send)


def per_device(q_rows, k_rows, v_rows, gate_rows, beta_logits, log_decay, norm_gain, out_weight, prompt_blocks, arrival_slot):
    smem = pl.BlockSpec(memory_space=pltpu.SMEM)
    vmem = pl.BlockSpec(memory_space=pltpu.VMEM)
    whole = pl.BlockSpec(memory_space=pl.ANY)
    tokens = LOCAL * SPAN
    dma = pltpu.SemaphoreType.DMA
    return pl.pallas_call(
        main_kernel,
        out_shape=pltpu.VMEM((tokens // PEERS, MODEL), BF16),
        in_specs=[smem, smem] + [whole] * 8,
        out_specs=vmem,
        scratch_shapes=[
            pltpu.VMEM((tokens, DK), BF16),
            pltpu.VMEM((tokens, DK), BF16),
            pltpu.VMEM((tokens, HEADS * DV), BF16),
            pltpu.VMEM((tokens, HEADS * DV), BF16),
            pltpu.VMEM((HEADS, tokens), BF16),
            pltpu.VMEM((HEADS, tokens), BF16),
            pltpu.VMEM((1, DV), F32),
            pltpu.VMEM((HEADS, LOCAL, DK, DK), BF16),
            pltpu.VMEM((HEADS, CHIPS, LOCAL + 1, SLICE, DK), BF16),
            pltpu.VMEM((HEADS, SLICE, DK), F32),
            pltpu.VMEM((HEADS, LOCAL, SPAN, DK), F32),
            pltpu.VMEM((HEADS, LOCAL, SPAN, DV), F32),
            pltpu.VMEM((1, SPAN), jnp.int32),
            pltpu.SMEM((1, SPAN), jnp.int32),
            pltpu.VMEM((BLOCKS, DK, DK), BF16),
            pltpu.VMEM((PEERS, LOCAL + 1, SLICE, DK), BF16),
            pltpu.VMEM((PEERS * 8, DK), F32),
            pltpu.VMEM((BLOCKS, SLICE, DK), BF16),
            pltpu.VMEM((BLOCKS, SLICE, DK), BF16),
            pltpu.VMEM((HEADS, LOCAL, DV, DK), BF16),
            pltpu.VMEM((LOCAL, SPAN, HEADS * DV), F32),
            pltpu.VMEM((LOCAL, SIDE, 32, HEADS * DV), BF16),
            pltpu.VMEM((2, SIDE, LOCAL, 32, HEADS * DV), BF16),
            pltpu.VMEM((2, SIDE, HEADS * DV, MODEL // 2), BF16),
            pltpu.VMEM((PIECES, SIDE, 32, PIECE), BF16),
            pltpu.VMEM((PIECES, SIDE, 32, PIECE), BF16),
            dma((7,)), dma, dma, dma, dma((2,)), dma, dma,
            dma, dma((2 * PEERS,)), dma, dma,
            dma, dma, dma, dma, dma, dma, dma, dma((PIECES,)),
        ],
        compiler_params=pltpu.CompilerParams(
            collective_id=0, has_side_effects=True, vmem_limit_bytes=VMEM_LIMIT
        ),
    )(
        arrival_slot, prompt_blocks, q_rows, k_rows, v_rows, gate_rows, beta_logits.T, log_decay.T,
        norm_gain.reshape(1, DV), out_weight,
    )


def solution(mesh):
    in_specs = (
        P("ctx", "head"),
        P("ctx", "head"),
        P("ctx", "head"),
        P("ctx", "head"),
        P("ctx", "head"),
        P("ctx", "head"),
        P(),
        P("head", None),
        P(),
        P(),
    )
    return jax.shard_map(
        per_device, mesh=mesh, in_specs=in_specs, out_specs=P(("ctx", "head"), None), check_vma=False
    )
```

```python
import jax
import jax.numpy as jnp
from jax import lax
from jax.experimental import pallas as pl
from jax.experimental.pallas import tpu as pltpu
from jax.sharding import PartitionSpec as P

SPAN = 128
DK = 128
DV = 128
HEADS = 2
LOCAL = 4
PEERS = 16
CHIPS = 8
SLICE = 16
BLOCKS = 64
CHAIN = 32
SIDE = 4
MODEL = 2048
PIECES = 4
PIECE = MODEL // PIECES
GROUP = 2
VMEM_LIMIT = 60 * 2**20
MESH = pl.DeviceIdType.MESH
F32 = jnp.float32
BF16 = jnp.bfloat16


def split(x):
    high = x.astype(BF16)
    return high, (x - high.astype(F32)).astype(BF16)


def mm(a, b):
    return jnp.dot(a, b, preferred_element_type=F32)


def mm_t(a, b):
    return lax.dot_general(a, b, (((1,), (1,)), ((), ())), preferred_element_type=F32)


def product(a, b):
    a_high, a_low = a
    b_high, b_low = b
    n = b_high.shape[1]
    if n == 128:
        left = jnp.concatenate([a_high, a_low], axis=1)
        right = jnp.concatenate(
            [
                jnp.concatenate([b_high, b_low], axis=1),
                jnp.concatenate([b_high, jnp.zeros_like(b_low)], axis=1),
            ],
            axis=0,
        )
        both = mm(left, right)
        return both[:, :n] + both[:, n:]
    left = jnp.concatenate([a_high, a_low], axis=1)
    right = jnp.concatenate([b_high, b_high], axis=0)
    return mm(left, right) + mm(a_high, b_low)


def spread_lanes(column):
    return jnp.broadcast_to(column, (column.shape[0], 128))


def block_terms(i, h, q, k, beta_row, decay_row, v, shared, consts):
    tri, strict, incl = consts
    qn, kf, kt2, rk_wide, kk, qk = shared
    beta = jnp.broadcast_to(1.0 / (1.0 + jnp.exp(-beta_row)), (SPAN, SPAN)).T
    steps = jnp.broadcast_to(decay_row, (SPAN, SPAN)).astype(BF16)
    wide = mm_t(tri, steps)
    wide_row = mm_t(steps, tri)
    ratio = jnp.exp(jnp.minimum(wide - wide_row, 0.0))
    lower = jnp.where(strict, beta * ratio * kk, 0.0)
    attend = jnp.where(incl, ratio * qk, 0.0)
    growth = jnp.exp(wide)
    end = wide[SPAN - 1 : SPAN, :]
    tail = jnp.exp(end - wide) * rk_wide
    rhs = jnp.concatenate([beta * v, beta * growth * rk_wide * kf], axis=1)
    return dict(i=i, h=h, lower=lower, attend=attend, tail=tail, rhs=rhs, kt2=kt2, grown=growth * qn, decay=jnp.exp(end))


def main_kernel(
    arr_ref, prompt_ref, q_hbm, k_hbm, v_hbm, gate_hbm, beta_hbm, decay_hbm, gain_hbm, w_ref,
    out_ref,
    q_ref, k_ref, v_ref, gate_ref, beta_ref, decay_ref, gain_ref,
    m_ref, o_ref, d_ref, ql_ref, lo_ref, inv_vmem, inv_ref,
    m_all, o_all, d_all, stream, states, entry, gated, normed, rows_all, w_all, part, got,
    in_sem, inv_sem, w_send, w_recv, w_local, c_send, c_recv, m_send, m_recv, o_send, o_recv,
    s_send, s_recv, n_send, n_recv, r_send, r_recv, p_send, p_recv,
):
    ctx = lax.axis_index("ctx")
    head = lax.axis_index("head")
    chip, core = lax.div(ctx, 2), lax.rem(ctx, 2)
    sibling = 2 * chip + 1 - core
    side_x, side_y = lax.div(head, SIDE), lax.rem(head, SIDE)

    def ctx_peer(k):
        return lax.rem(ctx + k, PEERS)

    def y_peer(k):
        return side_x * SIDE + lax.rem(side_y + k, SIDE)

    def x_peer(k):
        return lax.rem(side_x + k, SIDE) * SIDE + side_y

    barrier = pltpu.get_barrier_semaphore()

    loads = [
        pltpu.make_async_copy(src, dst, in_sem.at[n])
        for n, (src, dst) in enumerate(
            (
                (k_hbm, k_ref), (q_hbm, q_ref), (beta_hbm, beta_ref), (decay_hbm, decay_ref),
                (v_hbm, v_ref), (gate_hbm, gate_ref), (gain_hbm, gain_ref),
            )
        )
    ]
    for load in loads:
        load.start()
    for k in range(1, PEERS):
        pl.semaphore_signal(barrier, inc=1, device_id=(ctx_peer(k), head), device_id_type=MESH)
    for k in range(1, SIDE):
        pl.semaphore_signal(barrier, inc=1, device_id=(ctx, y_peer(k)), device_id_type=MESH)
        pl.semaphore_signal(barrier, inc=1, device_id=(ctx, x_peer(k)), device_id_type=MESH)

    def remote(src, dst, send, recv, target):
        return pltpu.make_async_remote_copy(
            src_ref=src, dst_ref=dst, send_sem=send, recv_sem=recv, device_id=target, device_id_type=MESH
        )

    def finish_sends(ref, sem):
        remote(ref, ref, sem, sem, (ctx, head)).wait_send()

    def finish_arrivals(ref, sem):
        remote(ref, ref, sem, sem, (ctx, head)).wait_recv()

    def o_copy(k):
        to = ctx_peer(k)
        return remote(o_ref.at[lax.rem(to, 2), lax.div(to, 2)], o_all.at[ctx], o_send, o_recv, (to, head))

    def m_slot(source, g):
        return m_all.at[pl.ds(LOCAL * source + GROUP * g, GROUP)]

    def m_near(z):
        return lax.rem(chip + z + CHIPS, CHIPS)

    def m_first(h, step, g):
        return remote(
            m_ref.at[h, pl.ds(GROUP * g, GROUP)], m_slot(ctx, g), m_send, m_recv.at[2 * ctx + g],
            (2 * m_near(step) + h, head),
        )

    def m_sibling(g):
        return remote(
            m_ref.at[1 - core, pl.ds(GROUP * g, GROUP)], m_slot(ctx, g), m_send, m_recv.at[2 * ctx + g],
            (sibling, head),
        )

    def m_next(source, g, step):
        return remote(
            m_slot(source, g), m_slot(source, g), m_send, m_recv.at[2 * source + g],
            (2 * m_near(step) + core, head),
        )

    def forward(k, g):
        for step in (1, -1):
            for s in range(2):
                last = 4 if (s == 0) == (step == 1) else 3
                if k > last:
                    continue
                source = 2 * m_near(-step * k) + s
                m_next(source, g, step).wait_recv()
                if k < last:
                    m_next(source, g, step).start()

    def attend_locally(chains):
        for c in chains:
            i, h = c["i"], c["h"]
            local = product(split(c["attend"]), split(c["solved"]))
            lo_ref[h, i] = local[:, :DV]
            ql_ref[h, i] = c["grown"] - local[:, DV:]

    def w_half(half):
        return w_ref.at[:, pl.ds(pl.multiple_of(half * (MODEL // 2), MODEL // 2), MODEL // 2)]

    def pick(over_x, over_y):
        return core * over_x + (1 - core) * over_y

    def w_copy(k):
        to = pick(x_peer(k), y_peer(k))
        return remote(w_half(core), w_all.at[core, pick(side_x, side_y)], w_send, w_recv, (ctx, to))

    def w_pass(k):
        slot = w_all.at[core, lax.rem(pick(side_x, side_y) + k, SIDE)]
        return remote(slot, slot, c_send, c_recv, (sibling, head))

    row = lax.broadcasted_iota(jnp.int32, (SPAN, SPAN), 0)
    col = lax.broadcasted_iota(jnp.int32, (SPAN, SPAN), 1)
    differ = row ^ col
    incl = row >= col
    strict = row > col
    tri = incl.astype(F32).astype(BF16)
    masks = [((differ >= s) & (differ < 2 * s)).astype(F32).astype(BF16) for s in (2, 4, 8, 16, 32, 64)]
    first = (differ == 1).astype(F32)
    eye = (row == col).astype(F32)
    d_ref[...] = jnp.zeros((HEADS, SLICE, DK), F32)
    everything = []

    for load in loads[:5]:
        load.wait()
    for g in range(LOCAL // GROUP):
        chains = []
        for i in range(g * GROUP, (g + 1) * GROUP):
            rows = pl.ds(i * SPAN, SPAN)
            q = q_ref[rows, :]
            k = k_ref[rows, :]
            qf = q.astype(F32)
            kf = k.astype(F32)
            rq = lax.rsqrt(jnp.sum(qf * qf, axis=-1, keepdims=True) + 1e-6) * DK**-0.5
            rk = lax.rsqrt(jnp.sum(kf * kf, axis=-1, keepdims=True) + 1e-6)
            rk_wide = spread_lanes(rk)
            rk_row = rk_wide.T
            both = mm_t(jnp.concatenate([k, q], axis=0), k)
            kk = both[:SPAN] * rk_wide * rk_row
            qk = both[SPAN:] * spread_lanes(rq) * rk_row
            kt = k.T
            shared = (qf * rq, kf, jnp.concatenate([kt, kt], axis=1), rk_wide, kk, qk)
            logits = beta_ref[:, rows].astype(F32)
            decays = decay_ref[:, rows].astype(F32)
            for h in range(HEADS):
                chains.append(
                    block_terms(
                        i, h, q, k, logits[h : h + 1], decays[h : h + 1],
                        v_ref[rows, h * DV : (h + 1) * DV].astype(F32), shared, (tri, strict, incl),
                    )
                )
        for c in chains:
            c["parts"] = split(c["lower"])
            c["inverse"] = eye - c["lower"] * first
        for mask in masks:
            for c in chains:
                c["halves"] = split(c["inverse"])
                off = (c["parts"][0] * mask, c["parts"][1] * mask)
                c["inner"] = product(off, c["halves"])
            for c in chains:
                c["inverse"] = c["inverse"] - product(c["halves"], split(c["inner"]))
        for c in chains:
            c["solved"] = product(split(c["inverse"]), split(c["rhs"]))
        for c in chains:
            tail2 = jnp.concatenate([c["tail"], c["tail"]], axis=1)
            high, low = split(tail2 * c["solved"])
            shift = mm(c["kt2"], jnp.concatenate([high, low], axis=0))
            i, h = c["i"], c["h"]
            m_ref[h, i] = shift[:, DV:].T.astype(BF16)
            o_ref[h, :, i] = shift[:, :DV].T.reshape(CHIPS, SLICE, DK).astype(BF16)
            decay = c["decay"].astype(BF16).astype(F32)
            d_ref[h, i : i + 1, :] = decay
            d_ref[h, 8 + i : 9 + i, :] = c["decay"] - decay
        everything += chains
        if g == 0:
            pl.semaphore_wait(barrier, PEERS - 1 + 2 * (SIDE - 1))
        for h, step in ((0, 1), (0, -1), (1, 1), (1, -1)):
            m_first(h, step, g).start()
        m_sibling(g).start()

    forward(1, 0)
    for h in range(HEADS):
        o_ref[h, :, LOCAL] = jnp.broadcast_to(d_ref[h].astype(BF16), (CHIPS, SLICE, DK))
    for k in range(1, PEERS):
        o_copy(k).start()
    m_all[pl.ds(LOCAL * ctx, LOCAL)] = m_ref[core]
    o_all[ctx] = o_ref[core, chip]
    attend_locally(everything[: len(everything) // 2])
    forward(1, 1)
    forward(2, 0)
    attend_locally(everything[len(everything) // 2 :])
    forward(2, 1)

    lanes = lax.broadcasted_iota(jnp.int32, (1, SPAN), 1)
    found = jnp.zeros((1, SPAN), jnp.int32)
    for t in range(BLOCKS):
        found = jnp.where(lanes == arr_ref[t], t, found)
    inv_vmem[...] = found
    inv_copy = pltpu.make_async_copy(inv_vmem, inv_ref, inv_sem)
    inv_copy.start()
    bits = jnp.int32(0)
    start = prompt_ref[0]
    for i in range(1, 7):
        bits = bits | (jnp.int32(1) << start)
        start = start + prompt_ref[i]

    forward(3, 0)
    forward(3, 1)
    for k in range(1, SIDE):
        w_copy(k).start()
    w_own = [
        pltpu.make_async_copy(w_half(half), w_all.at[half, side], w_local.at[half])
        for half, side in enumerate((side_y, side_x))
    ]
    for copy in w_own:
        copy.start()
    forward(4, 0)
    forward(4, 1)
    for g in range(LOCAL // GROUP):
        m_next(sibling, g, 0).wait_recv()
    finish_arrivals(o_all.at[pl.ds(0, PEERS - 1)], o_recv)
    for source in range(PEERS):
        tile = o_all[source, LOCAL].astype(F32)
        d_all[source * 8 : source * 8 + 8, :] = tile[:8] + tile[8:]
    inv_copy.wait()

    def advance(state, t):
        slot = arr_ref[t]
        stream[t] = state.astype(BF16)
        high, low = split(state)
        moved = mm(jnp.concatenate([high, low], axis=0), m_all[slot])
        source, i = lax.div(slot, LOCAL), lax.rem(slot, LOCAL)
        decay = d_all[pl.ds(source * 8 + i, 1), :]
        return decay * state + o_all[source, i].astype(F32) - (moved[:SLICE] + moved[SLICE:])

    def step(t, pair):
        keep = (1 - ((bits >> t) & 1)).astype(F32)
        return advance(keep * pair[0], t), advance(pair[1], t + CHAIN)

    empty = jnp.zeros((SLICE, DK), F32)
    lax.fori_loop(0, CHAIN, step, (empty, empty), unroll=32)

    def place(to):
        for i in range(LOCAL):
            a = LOCAL * to + i
            states[a] = stream[inv_ref[0, a]]

    def s_rows(h, z):
        return entry.at[h, :, pl.ds(pl.multiple_of(SLICE * z, SLICE), SLICE), :]

    def s_copy(k):
        to = ctx_peer(k)
        return remote(states.at[pl.ds(LOCAL * to, LOCAL)], s_rows(core, chip), s_send, s_recv, (to, head))

    for k in range(1, PEERS):
        place(ctx_peer(k))
        s_copy(k).start()
    place(ctx)
    entry[core, :, pl.ds(pl.multiple_of(SLICE * chip, SLICE), SLICE), :] = states[pl.ds(LOCAL * ctx, LOCAL)]
    for load in loads[5:]:
        load.wait()
    gain = jnp.concatenate([gain_ref[...]] * HEADS, axis=1)
    for i in range(LOCAL):
        gate = gate_ref[i * SPAN : (i + 1) * SPAN, :].astype(F32)
        gated[i] = gain * (gate / (1.0 + jnp.exp(-gate)))
    for copy in w_own:
        copy.wait()
    finish_arrivals(w_all.at[0, pl.ds(0, SIDE - 1)], w_recv)
    for k in range(1, SIDE):
        w_pass(k).start()
    finish_arrivals(states.at[pl.ds(0, LOCAL * (PEERS - 1))], s_recv)

    def n_copy(k, j):
        pair = pl.ds(GROUP * j, GROUP)
        return remote(
            normed.at[pair, lax.rem(side_y + k, SIDE)], rows_all.at[0, side_y, pair], n_send, n_recv, (ctx, y_peer(k))
        )

    def r_copy(i):
        return remote(normed.at[i], rows_all.at[1, side_x], r_send, r_recv, (ctx, i * SIDE + side_y))

    for i in range(LOCAL):
        for h in range(HEADS):
            high, low = split(ql_ref[h, i])
            state = entry[h, i]
            both = mm_t(jnp.concatenate([high, low], axis=0), state)
            core_out = both[:SPAN] + both[SPAN:] + lo_ref[h, i]
            scale = lax.rsqrt(jnp.mean(core_out * core_out, axis=-1, keepdims=True) + 1e-6)
            value = core_out * scale * gated[i, :, h * DV : (h + 1) * DV]
            normed[i, :, :, h * DV : (h + 1) * DV] = value.astype(BF16).reshape(SIDE, 32, DV)

        @pl.when(i != side_x)
        def _():
            r_copy(i).start()

        if i % GROUP == GROUP - 1:
            for k in range(1, SIDE):
                n_copy(k, i // GROUP).start()

    rows_all[0, side_y] = normed[:, side_y]
    rows_all[1, side_x] = normed[side_x]
    finish_arrivals(w_all.at[0, pl.ds(0, SIDE - 1)], c_recv)

    def p_copy(piece, k):
        if piece < PIECES // 2:
            source, to = lax.rem(side_x + k, SIDE), x_peer(k)
        else:
            source, to = lax.rem(side_y + k, SIDE), y_peer(k)
        return remote(
            part.at[piece, source], got.at[piece, k],
            p_send, p_recv.at[piece], (ctx, to),
        )

    order = list(range(PIECES // 2, PIECES)) + list(range(PIECES // 2))
    for piece in order:
        half, off = divmod(piece * PIECE, MODEL // 2)
        if off == 0:
            finish_arrivals(rows_all.at[half, pl.ds(0, SIDE - 1)], r_recv if half else n_recv)
            left = jnp.concatenate(
                [rows_all[half, n].reshape(SPAN, HEADS * DV) for n in range(SIDE)], axis=1
            )
        right = w_all[half, :, :, off : off + PIECE].reshape(SIDE * HEADS * DV, PIECE)
        total = mm(left, right)
        part[piece] = total.astype(BF16).reshape(SIDE, 32, PIECE)
        for k in range(1, SIDE):
            p_copy(piece, k).start()
    for piece in order:
        total = part[piece, side_x if piece < PIECES // 2 else side_y].astype(F32)
        finish_arrivals(got.at[piece, pl.ds(1, SIDE - 1)], p_recv.at[piece])
        for k in range(1, SIDE):
            total = total + got[piece, k].astype(F32)
        out_ref[:, piece * PIECE : (piece + 1) * PIECE] = total.astype(BF16)
    finish_sends(m_all.at[pl.ds(0, LOCAL * (PEERS - 1))], m_send)
    finish_sends(o_all.at[pl.ds(0, PEERS - 1)], o_send)
    finish_sends(states.at[pl.ds(0, LOCAL * (PEERS - 1))], s_send)
    finish_sends(w_all.at[0, pl.ds(0, SIDE - 1)], w_send)
    finish_sends(w_all.at[0, pl.ds(0, SIDE - 1)], c_send)
    finish_sends(rows_all.at[0, pl.ds(0, SIDE - 1)], n_send)
    finish_sends(rows_all.at[1, pl.ds(0, SIDE - 1)], r_send)
    finish_sends(part.at[pl.ds(0, PIECES - 1)], p_send)


def per_device(q_rows, k_rows, v_rows, gate_rows, beta_logits, log_decay, norm_gain, out_weight, prompt_blocks, arrival_slot):
    smem = pl.BlockSpec(memory_space=pltpu.SMEM)
    vmem = pl.BlockSpec(memory_space=pltpu.VMEM)
    whole = pl.BlockSpec(memory_space=pl.ANY)
    tokens = LOCAL * SPAN
    dma = pltpu.SemaphoreType.DMA
    return pl.pallas_call(
        main_kernel,
        out_shape=pltpu.VMEM((tokens // PEERS, MODEL), BF16),
        in_specs=[smem, smem] + [whole] * 8,
        out_specs=vmem,
        scratch_shapes=[
            pltpu.VMEM((tokens, DK), BF16),
            pltpu.VMEM((tokens, DK), BF16),
            pltpu.VMEM((tokens, HEADS * DV), BF16),
            pltpu.VMEM((tokens, HEADS * DV), BF16),
            pltpu.VMEM((HEADS, tokens), BF16),
            pltpu.VMEM((HEADS, tokens), BF16),
            pltpu.VMEM((1, DV), F32),
            pltpu.VMEM((HEADS, LOCAL, DK, DK), BF16),
            pltpu.VMEM((HEADS, CHIPS, LOCAL + 1, SLICE, DK), BF16),
            pltpu.VMEM((HEADS, SLICE, DK), F32),
            pltpu.VMEM((HEADS, LOCAL, SPAN, DK), F32),
            pltpu.VMEM((HEADS, LOCAL, SPAN, DV), F32),
            pltpu.VMEM((1, SPAN), jnp.int32),
            pltpu.SMEM((1, SPAN), jnp.int32),
            pltpu.VMEM((BLOCKS, DK, DK), BF16),
            pltpu.VMEM((PEERS, LOCAL + 1, SLICE, DK), BF16),
            pltpu.VMEM((PEERS * 8, DK), F32),
            pltpu.VMEM((BLOCKS, SLICE, DK), BF16),
            pltpu.VMEM((BLOCKS, SLICE, DK), BF16),
            pltpu.VMEM((HEADS, LOCAL, DV, DK), BF16),
            pltpu.VMEM((LOCAL, SPAN, HEADS * DV), F32),
            pltpu.VMEM((LOCAL, SIDE, 32, HEADS * DV), BF16),
            pltpu.VMEM((2, SIDE, LOCAL, 32, HEADS * DV), BF16),
            pltpu.VMEM((2, SIDE, HEADS * DV, MODEL // 2), BF16),
            pltpu.VMEM((PIECES, SIDE, 32, PIECE), BF16),
            pltpu.VMEM((PIECES, SIDE, 32, PIECE), BF16),
            dma((7,)), dma, dma, dma, dma((2,)), dma, dma,
            dma, dma((2 * PEERS,)), dma, dma,
            dma, dma, dma, dma, dma, dma, dma, dma((PIECES,)),
        ],
        compiler_params=pltpu.CompilerParams(
            collective_id=0, has_side_effects=True, vmem_limit_bytes=VMEM_LIMIT
        ),
    )(
        arrival_slot, prompt_blocks, q_rows, k_rows, v_rows, gate_rows, beta_logits.T, log_decay.T,
        norm_gain.reshape(1, DV), out_weight,
    )


def solution(mesh):
    in_specs = (
        P("ctx", "head"),
        P("ctx", "head"),
        P("ctx", "head"),
        P("ctx", "head"),
        P("ctx", "head"),
        P("ctx", "head"),
        P(),
        P("head", None),
        P(),
        P(),
    )
    return jax.shard_map(
        per_device, mesh=mesh, in_specs=in_specs, out_specs=P(("ctx", "head"), None), check_vma=False
    )
```
